128 devices in a mesh: seq: 8 (over z, core), exp: 16 (over x, y).
Axes of the slice: x: 4, y: 4, z: 4, core: 2. Of those that a mesh axis runs over, the one named last changes fastest.
Arguments:
- x_in: bfloat16 [16, 1024, 2048], P('exp', 'seq'), may hold values from -6 to 6
- dout: bfloat16 [16, 1024, 2048], P('exp', 'seq'), may hold values from -6 to 6
- route_ids: int32 [16, 1024, 2], P('exp', 'seq'), may hold values from 0 to 15, all different within a row; in each aligned block of 128 rows (0 to 127, 128 to 255, ..., all dimensions but the last counted through in order) at most 20 rows name the same one
- combine: float32 [16, 1024, 2], P('exp', 'seq'), may hold values from 0.2 to 1
- w_up: bfloat16 [16, 7168, 2048], P('exp', 'seq'), may hold values from -0.125 to 0.125
- w_down: bfloat16 [16, 7168, 2048], P('exp', 'seq'), may hold values from -0.0625 to 0.0625
- delta: float32 [16, 1024, 2048], P('exp', 'seq'), may hold values from 0.5 to 768, as said below
- rate: float32 [16, 2048], replicated, may hold values from 0.00028320312 to 0.031, as said below
- bmat: float32 [16, 1024, 16], P('exp', 'seq'), may hold values from -1.5 to 1.5
- cmat: float32 [16, 1024, 16], P('exp', 'seq'), may hold values from -0.375 to 0.375
Outputs:
- d_mid: bfloat16 [16, 1024, 2048], P('exp', 'seq')
- d_scan: bfloat16 [16, 1024, 2048], P('exp', 'seq')
The draws below stay inside these ranges and needn't reach their ends.
Inputs may be any that keep to these rules, and one draw needn't show every extreme that they name: `route_ids`: each row names 2 different experts; among the 128 rows of one device no expert is named more than 20 times, and in some devices one is named exactly 20 times. `delta`: positive. `rate`: positive.
All inputs are finite; a program needn't handle non-finite values.
Results may differ from the reference program's by a relative error of at most 0.012.
Values may be sent and summed in bfloat16 or wider, within the bound.
No kernel may reach another device: no remote copies, remote signals or barrier semaphores. Data moves between devices by JAX's collectives and lax.ppermute only.
A program may use at most 192 MiB of HBM per device.

```python
import math
from functools import partial
import jax
import jax.numpy as jnp
import numpy as np
from jax import lax

D = 2048
FF = 7168
NSTATE = 16
TOP = 2
TOK_DEV = 128
NEXP = 16
CAP = 20
SEQUENCE_COUNT = 16
SEQUENCE_LENGTH = 1024
N_SEQ = 8
N_EXP = 16


def draw_delta(key, part):
    key_one = jax.random.fold_in(key, 11)
    second_random_key = jax.random.fold_in(key, 12)
    baseline_steps = jnp.exp(jax.random.uniform(key_one, (SEQUENCE_COUNT, SEQUENCE_LENGTH, D), jnp.float32, math.log(0.5), math.log(2.0)))
    baseline_steps = jnp.clip(baseline_steps, 0.5, 2.0)
    spike_locations = jax.random.randint(second_random_key, (SEQUENCE_COUNT, 3), 0, SEQUENCE_LENGTH)
    position_index = jnp.arange(SEQUENCE_LENGTH, dtype=jnp.int32)
    spike_mask = jnp.any(spike_locations[:, :, None] == position_index[None, None, :], axis=1)
    spike_value = jnp.float32(3 * SEQUENCE_LENGTH // 4)
    return jnp.where(spike_mask[:, :, None], spike_value, baseline_steps).astype(jnp.float32)


def draw_rate(key, part):
    key_one = jax.random.fold_in(key, 21)
    second_random_key = jax.random.fold_in(key, 22)
    key_three = jax.random.fold_in(key, 23)
    slow_rates = jnp.exp(jax.random.uniform(key_one, (NSTATE, D), jnp.float32, math.log(0.3), math.log(0.6))) / SEQUENCE_LENGTH
    fast_rates = jnp.exp(jax.random.uniform(second_random_key, (NSTATE, D), jnp.float32, 0.0, math.log(0.03 * SEQUENCE_LENGTH))) / SEQUENCE_LENGTH
    slow_share = 0.5
    slow_pick = jax.random.uniform(key_three, (NSTATE, D), jnp.float32) < slow_share
    chosen = jnp.where(slow_pick, slow_rates, fast_rates)
    return jnp.clip(chosen, 0.3 / SEQUENCE_LENGTH, 0.03).astype(jnp.float32)


def block_scale(key, shape, shards, low, high):
    level, own = 1.0, jax.random.fold_in(key, 6)
    for axis_at, shards_of in shards:
        draws = jnp.exp(jax.random.uniform(jax.random.fold_in(own, axis_at), (shards_of,), jnp.float32, low / len(shards), high / len(shards)))
        level = level * jnp.repeat(draws, shape[axis_at] // shards_of).reshape([-1 if axis == axis_at else 1 for axis in range(len(shape))])
    return level


def routed_block(stream_key, own, number, rows, count, top, most, lean):
    sequence = jax.random.permutation(stream_key, count)
    heavy_load, usual = load_shares(count, rows * top, most, lean, True), load_shares(count, rows * top, most, lean, False)
    places = jnp.arange(count)

    def named(sizes, rotation):
        used = int((sizes > 0).sum())
        fixed = max(1, used // 4)
        shifted = fixed + (places - fixed + rotation * (used - fixed)) % max(1, count - fixed)
        return jnp.zeros((count,), jnp.int32).at[sequence[jnp.where(places < fixed, places, shifted)]].set(jnp.asarray(sizes, jnp.int32))

    sizes = jnp.where(number % 4 == 0, named(heavy_load, number // 4), named(usual, number - number // 4 - 1))
    mixed = jax.random.permutation(jax.random.fold_in(own, 3), count)
    donor, sink = mixed[0:count // 2 * 2:2], mixed[1:count // 2 * 2:2]
    slack = jnp.minimum(sizes[donor] - 1, most - sizes[sink]) // 2
    slack = jnp.where((donor == sequence[0]) | (sink == sequence[0]) | (sizes[sink] == 0), 0, jnp.maximum(slack, 0))
    shifted = jax.random.randint(jax.random.fold_in(own, 4), (count // 2,), 0, 1 << 20) % (slack + 1)
    sizes = sizes.at[donor].add(-shifted).at[sink].add(shifted)
    labels = jnp.searchsorted(jnp.cumsum(sizes), jnp.arange(rows * top), side="right").astype(jnp.int32)
    table = labels.reshape(top, rows).T
    table = table[jax.random.permutation(jax.random.fold_in(own, 1), rows)]
    rotation = jax.random.randint(jax.random.fold_in(own, 2), (rows, 1), 0, top)
    return jnp.take_along_axis(table, (jnp.arange(top)[None, :] + rotation) % top, axis=1)


def load_shares(count, total, limit, skew, full):
    portions = [(1 << 20) // math.isqrt(grade ** skew) + 1 for grade in range(1, count + 1)]
    largest = limit if full else min(limit, max(-(-total // count), total * portions[0] // sum(portions)))
    least = 1 if total - largest >= count - 1 else 0
    holding, rest = [largest] + [least] * (count - 1), total - largest - least * (count - 1)
    while rest > 0:
        movable = [i for i in range(1, count) if holding[i] < largest] or [i for i in range(1, count) if holding[i] < limit]
        whole, remaining = sum([portions[i] for i in movable]), rest
        for i in movable:
            addition = min(limit - holding[i], max(1, remaining * portions[i] // whole), rest)
            holding[i] = holding[i] + addition
            rest = rest - addition
    return np.array(holding)


def centred(own_key, extent, spread, limit, split=(), kind=jnp.bfloat16):
    entries = spread * jax.random.normal(own_key, extent, jnp.float32)
    if split:
        entries = entries * block_scale(own_key, extent, split, -0.22, 0.18)
    return jnp.clip(entries, -limit, limit).astype(kind)


def setup_inputs(seed: int = 0) -> dict:
    seeds = jax.random.split(jax.random.key(seed), 11)
    x_in = centred(seeds[0], (SEQUENCE_COUNT, SEQUENCE_LENGTH, D), 1.0, 6.0, ((0, 16), (1, 8)))
    dout = centred(seeds[1], (SEQUENCE_COUNT, SEQUENCE_LENGTH, D), 1.0, 6.0, ((0, 16), (1, 8)))
    route_ids_keys = jax.random.split(jax.random.fold_in(seeds[2], 1), SEQUENCE_COUNT * SEQUENCE_LENGTH // TOK_DEV)
    route_ids_turns = jax.random.permutation(jax.random.fold_in(seeds[2], 3), SEQUENCE_COUNT * SEQUENCE_LENGTH // TOK_DEV)
    route_ids = jax.vmap(lambda own, number: routed_block(jax.random.fold_in(seeds[2], 2), own, number, TOK_DEV, NEXP, TOP, CAP, 2))(route_ids_keys, route_ids_turns).reshape((SEQUENCE_COUNT, SEQUENCE_LENGTH, TOP))
    combine = jnp.clip(0.2 + 0.8 * jax.random.uniform(seeds[3], (SEQUENCE_COUNT, SEQUENCE_LENGTH, TOP), jnp.float32) ** block_scale(seeds[3], (SEQUENCE_COUNT, SEQUENCE_LENGTH, TOP), ((0, 16), (1, 8)), -0.2, 0.2), 0.2, 1.0)
    w_up = centred(seeds[4], (NEXP, FF, D), D ** -0.5, 0.125, ((0, 16), (1, 8)))
    w_down = centred(seeds[5], (NEXP, FF, D), FF ** -0.5, 0.0625, ((0, 16), (1, 8)))
    delta = draw_delta(jax.random.fold_in(seeds[10], 71), 0)
    rate = draw_rate(jax.random.fold_in(seeds[10], 71), 0)
    bmat = centred(seeds[8], (SEQUENCE_COUNT, SEQUENCE_LENGTH, NSTATE), 0.25, 1.5, ((0, 16), (1, 8)), jnp.float32)
    cmat = centred(seeds[9], (SEQUENCE_COUNT, SEQUENCE_LENGTH, NSTATE), (2.0 * SEQUENCE_LENGTH ** -0.5), 0.375, ((0, 16), (1, 8)), jnp.float32)
    return {"x_in": x_in, "dout": dout, "route_ids": route_ids, "combine": combine, "w_up": w_up, "w_down": w_down, "delta": delta, "rate": rate, "bmat": bmat, "cmat": cmat}


def slot_tables(route_rows, weights, experts, capacity):
    tokens = route_rows.shape[0]
    flat_ids = route_rows.reshape(-1).astype(jnp.int32)
    one_hot = (flat_ids[:, None] == jnp.arange(experts, dtype=jnp.int32)[None, :]).astype(jnp.int32)
    earlier = jnp.cumsum(one_hot, axis=0) - one_hot
    slot_ids = lax.optimization_barrier(jnp.sum(earlier * one_hot, axis=1))
    target = flat_ids * capacity + slot_ids
    places = jnp.arange(experts * capacity, dtype=jnp.int32)
    picked = (places[:, None] == target[None, :]).reshape(experts * capacity, tokens, -1).astype(jnp.float32)
    send_table = lax.optimization_barrier(jnp.sum(picked, axis=2))
    weigh_table = lax.optimization_barrier(jnp.sum(picked * weights[None, :, :], axis=2))
    return (send_table, weigh_table)

def hidden_grad(rows_x, rows_dy, up_block, down_block):
    pre_act = lax.dot_general(rows_x, up_block, (((1,), (1,)), ((), ())), preferred_element_type=jnp.float32)
    back_grad = lax.dot_general(rows_dy, down_block, (((1,), (1,)), ((), ())), preferred_element_type=jnp.float32)
    sig_pre = jax.nn.sigmoid(pre_act)
    return (back_grad * sig_pre * (1.0 + pre_act * (1.0 - sig_pre))).astype(jnp.bfloat16)

def input_part(grad_pre, up_block):
    return jnp.dot(grad_pre, up_block, preferred_element_type=jnp.float32).astype(jnp.bfloat16)

def one_expert(inputs):
    rows_x, rows_dy, up_whole, down_whole = inputs
    grad_pre = hidden_grad(rows_x, rows_dy, up_whole, down_whole)
    hidden_dev = FF // N_SEQ
    running = jnp.zeros((rows_x.shape[0], D), jnp.float32)
    for shard_index in range(N_SEQ):
        low_unit = shard_index * hidden_dev
        partial_rows = input_part(grad_pre[:, low_unit:low_unit + hidden_dev], up_whole[low_unit:low_unit + hidden_dev])
        running = running + lax.optimization_barrier(partial_rows).astype(jnp.float32)
    return running

def back_step(flowing, inputs):
    grad_t, steps_t, mix_t, drive_t, rate_table = inputs
    state_now = drive_t[:, :, None] * grad_t[:, None, :] + flowing
    scan_out = lax.optimization_barrier(jnp.sum(mix_t[:, :, None] * state_now, axis=1))
    decays = jnp.exp(-steps_t[:, None, :] * rate_table[None, :, :])
    return (decays * state_now, scan_out)

def reference(x_in, dout, route_ids, combine, w_up, w_down, delta, rate, bmat, cmat):
    blocks = N_SEQ * N_EXP
    x_blocks = x_in.reshape(blocks, TOK_DEV, D)
    dy_blocks = dout.reshape(blocks, TOK_DEV, D)
    id_blocks = route_ids.reshape(blocks, TOK_DEV, TOP)
    weight_blocks = combine.reshape(blocks, TOK_DEV, TOP)
    send_tables, weigh_tables = jax.vmap(partial(slot_tables, experts=NEXP, capacity=CAP))(id_blocks, weight_blocks)
    rows_x = jnp.einsum('bst,btd->bsd', send_tables, x_blocks.astype(jnp.float32)).astype(jnp.bfloat16)
    rows_dy = jnp.einsum('bst,btd->bsd', send_tables, dy_blocks.astype(jnp.float32)).astype(jnp.bfloat16)
    rows_x = rows_x.reshape(blocks, NEXP, CAP, D).transpose(1, 0, 2, 3).reshape(NEXP, blocks * CAP, D)
    rows_dy = rows_dy.reshape(blocks, NEXP, CAP, D).transpose(1, 0, 2, 3).reshape(NEXP, blocks * CAP, D)
    rows_dx = lax.map(one_expert, (rows_x, rows_dy, w_up, w_down))
    rows_dx = rows_dx.reshape(NEXP, blocks, CAP, D).transpose(1, 0, 2, 3).reshape(blocks, NEXP * CAP, D)
    routed_grad = jnp.einsum('bst,bsd->btd', weigh_tables, rows_dx, precision=lax.Precision.HIGHEST)
    d_mid = (dy_blocks.astype(jnp.float32) + routed_grad).astype(jnp.bfloat16).reshape(SEQUENCE_COUNT, SEQUENCE_LENGTH, D)
    grad_mid = d_mid.astype(jnp.float32)
    rate_steps = jnp.broadcast_to(rate[None], (SEQUENCE_LENGTH,) + rate.shape)
    start_flow = jnp.zeros((SEQUENCE_COUNT, NSTATE, D), jnp.float32)
    final_flow, scan_outs = lax.scan(back_step, start_flow, (jnp.swapaxes(grad_mid, 0, 1), jnp.swapaxes(delta, 0, 1), jnp.swapaxes(bmat, 0, 1), jnp.swapaxes(cmat, 0, 1), rate_steps), reverse=True)
    d_scan = jnp.swapaxes(scan_outs, 0, 1).astype(jnp.bfloat16)
    return (d_mid, d_scan)
```

```python
import functools

import jax
import jax.numpy as jnp
import numpy as np
from jax import lax
from jax.experimental import pallas as pl
from jax.experimental.pallas import tpu as pltpu
from jax.sharding import Mesh
from jax.sharding import PartitionSpec as P

VMEM_LIMIT = 56 * 1024 * 1024
PAD = 24
CORES = 2
HIDDEN_STEP = 128
SCAN_COLS = 1024
BF = jnp.bfloat16
F32 = jnp.float32


def params():
    return pltpu.CompilerParams(vmem_limit_bytes=VMEM_LIMIT)


def whole(*shape):
    return pl.BlockSpec(shape, lambda *_: (0,) * len(shape))


def gather_body(experts, ids_ref, x_ref, dy_ref, xs_ref, dys_ref):
    tokens = x_ref.shape[0]
    ids = ids_ref[...]
    at = lax.broadcasted_iota(jnp.int32, (experts, tokens), 0)
    hots = [(at == ids[k : k + 1, :]).astype(F32) for k in range(2)]
    before = (
        lax.broadcasted_iota(jnp.int32, (tokens, tokens), 0)
        < lax.broadcasted_iota(jnp.int32, (tokens, tokens), 1)
    ).astype(F32)
    earlier = jnp.dot(
        (hots[0] + hots[1]).astype(BF), before.astype(BF), preferred_element_type=F32
    )
    place = lax.broadcasted_iota(jnp.int32, (experts * PAD, tokens), 0)
    pick = None
    for k in range(2):
        slot = jnp.sum(earlier * hots[k], axis=0, keepdims=True).astype(jnp.int32)
        hit = place == ids[k : k + 1, :] * PAD + slot
        pick = hit if pick is None else pick | hit
    table = pick.astype(F32).astype(BF)
    xs_ref[...] = jnp.dot(table, x_ref[...], preferred_element_type=F32).astype(BF)
    dys_ref[...] = jnp.dot(table, dy_ref[...], preferred_element_type=F32).astype(BF)


def gather_rows(ids_t, x, dy, experts):
    rows, dim = experts * PAD, x.shape[1]
    return pl.pallas_call(
        functools.partial(gather_body, experts),
        out_shape=[jax.ShapeDtypeStruct((rows, dim), BF)] * 2,
        compiler_params=params(),
        name="gather_rows",
    )(ids_t, x, dy)


def expert_body(pieces, *refs):
    xs, dys = refs[:pieces], refs[pieces : 2 * pieces]
    up_a, up_b, down_a, down_b = refs[2 * pieces : 2 * pieces + 4]
    outs = refs[2 * pieces + 4 : 3 * pieces + 4]
    x_all, dy_all, total = refs[3 * pieces + 4 :]
    step = pl.program_id(0)

    @pl.when(step == 0)
    def _():
        low = 0
        for x_ref, dy_ref in zip(xs, dys):
            size = x_ref.shape[0]
            x_all[low : low + size] = x_ref[...]
            dy_all[low : low + size] = dy_ref[...]
            low += size

    up = jnp.concatenate([up_a[...], up_b[...]], axis=0)
    down = jnp.concatenate([down_a[...], down_b[...]], axis=0)
    across = (((1,), (1,)), ((), ()))
    pre = lax.dot_general(x_all[...], up, across, preferred_element_type=F32)
    back = lax.dot_general(dy_all[...], down, across, preferred_element_type=F32)
    sig = jax.nn.sigmoid(pre)
    grad = (back * sig * (1.0 + pre * (1.0 - sig))).astype(BF)
    part = jnp.dot(grad, up, preferred_element_type=F32)

    @pl.when(step == 0)
    def _():
        total[...] = part

    @pl.when(step > 0)
    def _():
        total[...] += part

    @pl.when(step == pl.num_programs(0) - 1)
    def _():
        low = 0
        for out in outs:
            size = out.shape[0]
            out[...] = total[low : low + size].astype(BF)
            low += size


def expert_rows(xs, dys, weights):
    pieces = len(xs)
    dim = xs[0].shape[1]
    hidden = weights[0].shape[0]
    rows = sum(x.shape[0] for x in xs)
    tile = pl.BlockSpec((HIDDEN_STEP, dim), lambda i: (i, 0))
    return pl.pallas_call(
        functools.partial(expert_body, pieces),
        grid=(hidden // HIDDEN_STEP,),
        in_specs=[whole(*x.shape) for x in (*xs, *dys)] + [tile] * 4,
        out_specs=[whole(*x.shape) for x in xs],
        out_shape=[jax.ShapeDtypeStruct(x.shape, BF) for x in xs],
        scratch_shapes=[
            pltpu.VMEM((rows, dim), BF),
            pltpu.VMEM((rows, dim), BF),
            pltpu.VMEM((rows, dim), F32),
        ],
        compiler_params=params(),
        cost_estimate=pl.CostEstimate(
            flops=6 * rows * 2 * hidden * dim,
            bytes_accessed=2 * (4 * hidden * dim + 3 * rows * dim),
            transcendentals=rows * 2 * hidden,
        ),
        name="expert_rows",
    )(*xs, *dys, *weights)


def weigh_pair(ids, weights, experts):
    tokens = ids.shape[0]
    at = lax.broadcasted_iota(jnp.int32, (tokens, experts), 1)
    hots = [(at == ids[:, k : k + 1]).astype(F32) for k in range(2)]
    before = (
        lax.broadcasted_iota(jnp.int32, (tokens, tokens), 1)
        < lax.broadcasted_iota(jnp.int32, (tokens, tokens), 0)
    ).astype(F32)
    earlier = jnp.dot(
        before.astype(BF), (hots[0] + hots[1]).astype(BF), preferred_element_type=F32
    )
    place = lax.broadcasted_iota(jnp.int32, (tokens, experts * PAD), 1)
    table = jnp.zeros((tokens, experts * PAD), F32)
    for k in range(2):
        slot = jnp.sum(earlier * hots[k], axis=1, keepdims=True).astype(jnp.int32)
        hit = place == ids[:, k : k + 1] * PAD + slot
        table = table + jnp.where(hit, weights[:, k : k + 1], 0.0)
    high = table.astype(BF)
    low = (table - high.astype(F32)).astype(BF)
    return high, low


def scan_body(
    experts,
    ids_ref,
    weights_ref,
    back_ref,
    dout_ref,
    delta_ref,
    rate_ref,
    mix_ref,
    drive_ref,
    mid_ref,
    local_ref,
    start_ref,
    grad,
):
    high, low = weigh_pair(ids_ref[...], weights_ref[...], experts)
    back = back_ref[...]
    routed = jnp.dot(high, back, preferred_element_type=F32)
    routed += jnp.dot(low, back, preferred_element_type=F32)
    mid = (dout_ref[...].astype(F32) + routed).astype(BF)
    mid_ref[...] = mid
    grad[...] = mid.astype(F32)
    negative = -rate_ref[...]
    tokens, cols = grad.shape
    states = negative.shape[0]
    lanes = mix_ref.shape[2]
    repeat = cols // lanes

    def block(i, flow):
        low_t = pl.multiple_of((tokens // 8 - 1 - i) * 8, 8)
        grads = grad[pl.ds(low_t, 8)]
        deltas = delta_ref[pl.ds(low_t, 8)]
        rows = []
        for r in reversed(range(8)):
            drive = jnp.concatenate([drive_ref[low_t + r]] * repeat, axis=1)
            mix = jnp.concatenate([mix_ref[low_t + r]] * repeat, axis=1)
            state = drive * jnp.broadcast_to(grads[r : r + 1], (states, cols)) + flow
            rows.append(jnp.sum(mix * state, axis=0, keepdims=True))
            decay = jnp.exp(jnp.broadcast_to(deltas[r : r + 1], (states, cols)) * negative)
            flow = decay * state
        local_ref[pl.ds(low_t, 8)] = jnp.concatenate(rows[::-1], axis=0)
        return flow

    start_ref[...] = lax.fori_loop(
        0, tokens // 8, block, jnp.zeros((states, cols), F32)
    ).astype(BF)


def combine_and_scan(ids, weights, back, dout, delta, rate, mix, drive, experts):
    tokens, dim = dout.shape
    states = rate.shape[0]
    cols = SCAN_COLS

    def strip(rows):
        return pl.BlockSpec((rows, cols), lambda i: (0, i))

    return pl.pallas_call(
        functools.partial(scan_body, experts),
        grid=(dim // cols,),
        in_specs=[
            whole(*ids.shape),
            whole(*weights.shape),
            strip(back.shape[0]),
            strip(tokens),
            strip(tokens),
            strip(states),
            whole(*mix.shape),
            whole(*drive.shape),
        ],
        out_specs=[strip(tokens), strip(tokens), strip(states)],
        out_shape=[
            jax.ShapeDtypeStruct((tokens, dim), BF),
            jax.ShapeDtypeStruct((tokens, dim), F32),
            jax.ShapeDtypeStruct((states, dim), BF),
        ],
        scratch_shapes=[pltpu.VMEM((tokens, cols), F32)],
        compiler_params=params(),
        name="combine_and_scan",
    )(ids, weights, back, dout, delta, rate, mix, drive)


def carry_body(place_ref, starts_ref, totals_ref, rate_ref, local_ref, delta_ref, mix_ref, out_ref):
    place = place_ref[0]
    negative = -rate_ref[...]
    tokens, cols = local_ref.shape
    states = negative.shape[0]
    repeat = cols // mix_ref.shape[2]
    blocks = starts_ref.shape[0]
    flow = jnp.zeros((states, cols), F32)
    for at in reversed(range(blocks)):
        passed = jnp.exp(totals_ref[at : at + 1] * negative) * flow
        flow = jnp.where(at > place, starts_ref[at].astype(F32) + passed, flow)

    def block(i, flow):
        low_t = pl.multiple_of((tokens // 16 - 1 - i) * 16, 16)
        deltas = delta_ref[pl.ds(low_t, 16)]
        rows = []
        for r in reversed(range(16)):
            mix = jnp.concatenate([mix_ref[low_t + r]] * repeat, axis=1)
            rows.append(jnp.sum(mix * flow, axis=0, keepdims=True))
            decay = jnp.exp(jnp.broadcast_to(deltas[r : r + 1], (states, cols)) * negative)
            flow = decay * flow
        sums = jnp.concatenate(rows[::-1], axis=0)
        out_ref[pl.ds(low_t, 16)] = (local_ref[pl.ds(low_t, 16)] + sums).astype(BF)
        return flow

    lax.fori_loop(0, tokens // 16, block, flow)


def add_carry(place, starts, totals, rate, local, delta, mix):
    tokens, dim = local.shape
    states = rate.shape[0]
    blocks = starts.shape[0]
    cols = SCAN_COLS

    def strip(rows):
        return pl.BlockSpec((rows, cols), lambda i: (0, i))

    return pl.pallas_call(
        carry_body,
        grid=(dim // cols,),
        in_specs=[
            pl.BlockSpec(memory_space=pltpu.SMEM),
            pl.BlockSpec((blocks, states, cols), lambda i: (0, 0, i)),
            strip(blocks),
            strip(states),
            strip(tokens),
            strip(tokens),
            whole(*mix.shape),
        ],
        out_specs=strip(tokens),
        out_shape=jax.ShapeDtypeStruct((tokens, dim), BF),
        compiler_params=params(),
        name="add_carry",
    )(place, starts, totals, rate, local, delta, mix)


def on_device(z_size, capacity, x_in, dout, route_ids, combine, w_up, w_down, delta, rate, bmat, cmat):
    experts = lax.axis_size("exp")
    x, dy, ids, weights = x_in[0], dout[0], route_ids[0], combine[0]
    dim = x.shape[1]
    rows = experts * capacity
    half = rows // 2
    up, down = w_up[0], w_down[0]

    def shift(value, by):
        ring = [(i, (i + by) % z_size) for i in range(z_size)]
        return lax.ppermute(value, "z", ring)

    def swap(value):
        return lax.ppermute(value, "core", [(0, 1), (1, 0)])

    def exchange(value):
        return lax.all_to_all(
            value.reshape(experts, PAD, dim), "exp", split_axis=0, concat_axis=0, tiled=True
        ).reshape(experts * PAD, dim)

    both = (up, swap(up), down, swap(down))

    squeeze = np.zeros((rows, experts * PAD), np.float32)
    at = np.arange(rows)
    squeeze[at, at // capacity * PAD + at % capacity] = 1.0
    squeeze = jnp.asarray(squeeze, BF)

    x_send, dy_send = gather_rows(ids.T, x, dy, experts)
    x_own = jnp.dot(squeeze, exchange(x_send), preferred_element_type=F32).astype(BF)
    dy_own = jnp.dot(squeeze, exchange(dy_send), preferred_element_type=F32).astype(BF)

    x_prev, x_next = shift(x_own, 1), shift(x_own, -1)
    dy_prev, dy_next = shift(dy_own, 1), shift(dy_own, -1)
    x_far = (shift(x_prev[:half], 1), shift(x_next[half:], -1))
    dy_far = (shift(dy_prev[:half], 1), shift(dy_next[half:], -1))

    (part_own,) = expert_rows((x_own,), (dy_own,), both)
    part_prev, part_next = expert_rows((x_prev, x_next), (dy_prev, dy_next), both)
    far_low, far_high = expert_rows(x_far, dy_far, both)

    def plus(a, b):
        return (a.astype(F32) + b.astype(F32)).astype(BF)

    got_low, got_high = shift(far_low, 1), shift(far_high, -1)
    to_next = jnp.concatenate([plus(part_next[:half], got_low), part_next[half:]], axis=0)
    to_prev = jnp.concatenate([part_prev[:half], plus(part_prev[half:], got_high)], axis=0)
    from_prev, from_next = shift(to_next, 1), shift(to_prev, -1)
    summed = (
        part_own.astype(F32) + from_prev.astype(F32) + from_next.astype(F32)
    ).astype(BF)
    spread = jnp.dot(squeeze.T, summed, preferred_element_type=F32).astype(BF)
    back = exchange(spread)

    lanes = (delta.shape[1], bmat.shape[2], 128)
    mix = jnp.broadcast_to(bmat[0][:, :, None], lanes)
    drive = jnp.broadcast_to(cmat[0][:, :, None], lanes)
    steps = delta[0]
    totals = lax.all_gather(jnp.sum(steps, axis=0), ("z", "core"))
    mid, local, start = combine_and_scan(
        ids, weights, back, dy, steps, rate, mix, drive, experts
    )
    starts = lax.all_gather(start, ("z", "core"))
    place = lax.axis_index(("z", "core")).astype(jnp.int32).reshape(1)
    scan = add_carry(place, starts, totals, rate, local, steps, mix)
    return (mid[None], scan[None])


def solution(mesh):
    seq, exp = mesh.shape["seq"], mesh.shape["exp"]
    z_size = seq // CORES
    split = Mesh(mesh.devices.reshape(z_size, CORES, exp), ("z", "core", "exp"))
    token = P("exp", ("z", "core"), None)

    def run(x_in, dout, route_ids, *rest):
        tokens = route_ids.shape[1] // seq
        capacity = 5 * tokens * route_ids.shape[2] // (4 * exp)
        return jax.shard_map(
            functools.partial(on_device, z_size, capacity),
            mesh=split,
            in_specs=(token,) * 7 + (P(),) + (token,) * 2,
            out_specs=(token, token),
            check_vma=False,
        )(x_in, dout, route_ids, *rest)

    return run
```

```python
import functools

import jax
import jax.numpy as jnp
import numpy as np
from jax import lax
from jax.experimental import pallas as pl
from jax.experimental.pallas import tpu as pltpu
from jax.sharding import Mesh
from jax.sharding import PartitionSpec as P

VMEM_LIMIT = 56 * 1024 * 1024
CORES = 2
SIDE = 4
GROUP = 4
HIDDEN_STEP = 128
OUT_COLS = 1024
SCAN_COLS = 1024
BF = jnp.bfloat16
F32 = jnp.float32
SHIFTS = (
    (0, 0), (1, 0), (0, 1), (3, 0),
    (0, 3), (1, 1), (3, 3), (1, 3),
    (3, 1), (2, 0), (0, 2), (2, 1),
    (1, 2), (2, 3), (3, 2), (2, 2),
)


def params():
    return pltpu.CompilerParams(vmem_limit_bytes=VMEM_LIMIT)


def whole(*shape):
    return pl.BlockSpec(shape, lambda *_: (0,) * len(shape))


def tie(*values):
    return lax.optimization_barrier(values)


def gather_body(capacity, ids_ref, order_ref, x_ref, dy_ref, *outs):
    tokens = x_ref.shape[0]
    experts = len(outs)
    ids = ids_ref[...]
    order = jnp.broadcast_to(order_ref[...], (experts, tokens))
    hots = [(order == ids[k : k + 1, :]).astype(F32) for k in range(2)]
    before = (
        lax.broadcasted_iota(jnp.int32, (tokens, tokens), 0)
        < lax.broadcasted_iota(jnp.int32, (tokens, tokens), 1)
    ).astype(F32)
    earlier = jnp.dot(
        (hots[0] + hots[1]).astype(BF), before.astype(BF), preferred_element_type=F32
    )
    message = 2 * capacity
    base = lax.broadcasted_iota(jnp.int32, (experts, tokens), 0).astype(F32) * message
    place = lax.broadcasted_iota(jnp.int32, (experts * message, tokens), 0)
    pick_x = pick_dy = None
    for k in range(2):
        target = jnp.sum((earlier + base) * hots[k], axis=0, keepdims=True).astype(jnp.int32)
        hit_x, hit_dy = place == target, place == target + capacity
        pick_x = hit_x if pick_x is None else pick_x | hit_x
        pick_dy = hit_dy if pick_dy is None else pick_dy | hit_dy
    rows = jnp.dot(pick_x.astype(F32).astype(BF), x_ref[...], preferred_element_type=F32)
    rows += jnp.dot(pick_dy.astype(F32).astype(BF), dy_ref[...], preferred_element_type=F32)
    rows = rows.astype(BF)
    for p, out in enumerate(outs):
        out[...] = rows[p * message : (p + 1) * message]


def gather_rows(ids_t, order, x, dy, capacity):
    experts, dim = order.shape[0], x.shape[1]
    return pl.pallas_call(
        functools.partial(gather_body, capacity),
        out_shape=[jax.ShapeDtypeStruct((2 * capacity, dim), BF)] * experts,
        compiler_params=params(),
        name="gather_rows",
    )(ids_t, order, x, dy)


def sort_body(table_ref, *refs):
    ins, out = refs[:-1], refs[-1]
    rows = jnp.concatenate([r[...] for r in ins], axis=0)
    out[...] = jnp.dot(table_ref[...], rows, preferred_element_type=F32).astype(BF)


def sort_messages(messages, capacity):
    count, dim = len(messages), messages[0].shape[1]
    rows = 2 * capacity * count
    at = np.arange(rows)
    kind, rest = at // (capacity * count), at % (capacity * count)
    table = np.zeros((rows, rows), np.float32)
    table[at, rest // capacity * 2 * capacity + kind * capacity + rest % capacity] = 1.0
    return pl.pallas_call(
        sort_body,
        out_shape=jax.ShapeDtypeStruct((rows, dim), BF),
        compiler_params=params(),
        name="sort_messages",
    )(jnp.asarray(table, BF), *messages)


def pack_body(table_ref, own_a, own_b, prev_ref, next_ref, *outs):
    half = own_a.shape[0]
    sums = []
    for own, low in ((own_a, 0), (own_b, half)):
        total = own[...].astype(F32) + prev_ref[low : low + half].astype(F32)
        sums.append((total + next_ref[low : low + half].astype(F32)).astype(BF))
    rows = jnp.dot(
        table_ref[...], jnp.concatenate(sums, axis=0), preferred_element_type=F32
    ).astype(BF)
    size = outs[0].shape[0]
    for p, out in enumerate(outs):
        out[...] = rows[p * size : (p + 1) * size]


def pack_returns(own_a, own_b, from_prev, from_next, capacity):
    rows, dim = from_prev.shape
    count = rows // capacity
    size = -(-capacity // 8) * 8
    table = np.zeros((count * size, rows), np.float32)
    at = np.arange(rows)
    table[at // capacity * size + at % capacity, at] = 1.0
    return pl.pallas_call(
        pack_body,
        out_shape=[jax.ShapeDtypeStruct((size, dim), BF)] * count,
        compiler_params=params(),
        name="pack_returns",
    )(jnp.asarray(table, BF), own_a, own_b, from_prev, from_next)


def hop_body(next_a, next_b, prev_a, prev_b, got_a, got_b, to_next, to_prev):
    half = next_a.shape[0]
    to_next[:half] = (next_a[...].astype(F32) + got_a[...].astype(F32)).astype(BF)
    to_next[half:] = next_b[...]
    to_prev[:half] = prev_a[...]
    to_prev[half:] = (prev_b[...].astype(F32) + got_b[...].astype(F32)).astype(BF)


def hop_sums(*parts):
    half, dim = parts[0].shape
    return pl.pallas_call(
        hop_body,
        out_shape=[jax.ShapeDtypeStruct((2 * half, dim), BF)] * 2,
        compiler_params=params(),
        name="hop_sums",
    )(*parts)


def expert_body(pieces, steps, *refs):
    ins = refs[:pieces]
    up_a, up_b, down_a, down_b = refs[pieces : pieces + 4]
    outs = refs[pieces + 4 : 2 * pieces + 4]
    x_all, dy_all, up_all, grads = refs[2 * pieces + 4 :]
    step = pl.program_id(0)
    size = outs[0].shape[0]
    width = 2 * up_a.shape[0]

    @pl.when(step == 0)
    def _():
        for i, piece in enumerate(ins):
            x_all[i * size : (i + 1) * size] = piece[:size]
            dy_all[i * size : (i + 1) * size] = piece[size:]

    @pl.when(step < steps)
    def _():
        up = jnp.concatenate([up_a[...], up_b[...]], axis=0)
        down = jnp.concatenate([down_a[...], down_b[...]], axis=0)
        up_all[pl.ds(pl.multiple_of(step * width, width), width)] = up
        across = (((1,), (1,)), ((), ()))
        pre = lax.dot_general(x_all[...], up, across, preferred_element_type=F32)
        back = lax.dot_general(dy_all[...], down, across, preferred_element_type=F32)
        sig = jax.nn.sigmoid(pre)
        grads[step] = (back * sig * (1.0 + pre * (1.0 - sig))).astype(BF)

    @pl.when(step >= steps)
    def _():
        grad = jnp.concatenate([grads[i] for i in range(steps)], axis=1)
        cols = outs[0].shape[1]
        at = pl.ds(pl.multiple_of((step - steps) * cols, cols), cols)
        part = jnp.dot(grad, up_all[:, at], preferred_element_type=F32).astype(BF)
        for i, out in enumerate(outs):
            out[...] = part[i * size : (i + 1) * size]


def expert_rows(ins, weights):
    pieces = len(ins)
    both, dim = ins[0].shape
    size = both // 2
    rows = pieces * size
    hidden = weights[0].shape[0]
    steps = hidden // HIDDEN_STEP
    tile = pl.BlockSpec((HIDDEN_STEP, dim), lambda i: (jnp.minimum(i, steps - 1), 0))
    return pl.pallas_call(
        functools.partial(expert_body, pieces, steps),
        grid=(steps + dim // OUT_COLS,),
        in_specs=[whole(both, dim)] * pieces + [tile] * 4,
        out_specs=[
            pl.BlockSpec((size, OUT_COLS), lambda i: (0, jnp.maximum(i - steps, 0)))
        ]
        * pieces,
        out_shape=[jax.ShapeDtypeStruct((size, dim), BF)] * pieces,
        scratch_shapes=[
            pltpu.VMEM((rows, dim), BF),
            pltpu.VMEM((rows, dim), BF),
            pltpu.VMEM((2 * hidden, dim), BF),
            pltpu.VMEM((steps, rows, 2 * HIDDEN_STEP), BF),
        ],
        compiler_params=params(),
        cost_estimate=pl.CostEstimate(
            flops=6 * rows * 2 * hidden * dim,
            bytes_accessed=2 * (4 * hidden * dim + 3 * rows * dim),
            transcendentals=rows * 2 * hidden,
        ),
        name="expert_rows",
    )(*ins, *weights)


def weigh_pair(ids, order, weights, padded):
    tokens = ids.shape[0]
    experts = order.shape[1]
    order = jnp.broadcast_to(order, (tokens, experts))
    hots = [(order == ids[:, k : k + 1]).astype(F32) for k in range(2)]
    before = (
        lax.broadcasted_iota(jnp.int32, (tokens, tokens), 1)
        < lax.broadcasted_iota(jnp.int32, (tokens, tokens), 0)
    ).astype(F32)
    earlier = jnp.dot(
        before.astype(BF), (hots[0] + hots[1]).astype(BF), preferred_element_type=F32
    )
    base = lax.broadcasted_iota(jnp.int32, (tokens, experts), 1).astype(F32) * padded
    place = lax.broadcasted_iota(jnp.int32, (tokens, experts * padded), 1)
    table = jnp.zeros((tokens, experts * padded), F32)
    for k in range(2):
        target = jnp.sum((earlier + base) * hots[k], axis=1, keepdims=True).astype(jnp.int32)
        table = table + jnp.where(place == target, weights[:, k : k + 1], 0.0)
    high = table.astype(BF)
    low = (table - high.astype(F32)).astype(BF)
    return high, low


def scan_body(experts, ids_ref, order_ref, weights_ref, *refs):
    backs = refs[:experts]
    dout_ref, delta_ref, rate_ref, mix_ref, drive_ref = refs[experts : experts + 5]
    mid_ref, local_ref, start_ref, grad = refs[experts + 5 :]
    high, low = weigh_pair(
        ids_ref[...], order_ref[...], weights_ref[...], backs[0].shape[0]
    )
    back = jnp.concatenate([b[...] for b in backs], axis=0)
    routed = jnp.dot(high, back, preferred_element_type=F32)
    routed += jnp.dot(low, back, preferred_element_type=F32)
    mid = (dout_ref[...].astype(F32) + routed).astype(BF)
    mid_ref[...] = mid
    grad[...] = mid.astype(F32)
    negative = -rate_ref[...]
    tokens, cols = grad.shape
    states = negative.shape[0]
    repeat = cols // mix_ref.shape[2]

    def block(i, flow):
        low_t = pl.multiple_of((tokens // 8 - 1 - i) * 8, 8)
        grads = grad[pl.ds(low_t, 8)]
        deltas = delta_ref[pl.ds(low_t, 8)]
        rows = []
        for r in reversed(range(8)):
            drive = jnp.concatenate([drive_ref[low_t + r]] * repeat, axis=1)
            mix = jnp.concatenate([mix_ref[low_t + r]] * repeat, axis=1)
            state = drive * jnp.broadcast_to(grads[r : r + 1], (states, cols)) + flow
            rows.append(jnp.sum(mix * state, axis=0, keepdims=True))
            decay = jnp.exp(jnp.broadcast_to(deltas[r : r + 1], (states, cols)) * negative)
            flow = decay * state
        local_ref[pl.ds(low_t, 8)] = jnp.concatenate(rows[::-1], axis=0)
        return flow

    start_ref[...] = lax.fori_loop(
        0, tokens // 8, block, jnp.zeros((states, cols), F32)
    ).astype(BF)


def strip(rows, cols):
    return pl.BlockSpec((rows, cols), lambda i: (0, i))


def combine_and_scan(ids, order, weights, backs, dout, delta, rate, mix, drive):
    tokens, dim = dout.shape
    states = rate.shape[0]
    cols = SCAN_COLS
    return pl.pallas_call(
        functools.partial(scan_body, len(backs)),
        grid=(dim // cols,),
        in_specs=[whole(*ids.shape), whole(*order.shape), whole(*weights.shape)]
        + [strip(b.shape[0], cols) for b in backs]
        + [
            strip(tokens, cols),
            strip(tokens, cols),
            strip(states, cols),
            whole(*mix.shape),
            whole(*drive.shape),
        ],
        out_specs=[strip(tokens, cols), strip(tokens, cols), strip(states, cols)],
        out_shape=[
            jax.ShapeDtypeStruct((tokens, dim), BF),
            jax.ShapeDtypeStruct((tokens, dim), F32),
            jax.ShapeDtypeStruct((states, dim), BF),
        ],
        scratch_shapes=[pltpu.VMEM((tokens, cols), F32)],
        compiler_params=params(),
        name="combine_and_scan",
    )(ids, order, weights, *backs, dout, delta, rate, mix, drive)


def reach_body(delta_ref, rate_ref, mix_ref, reach_ref, total_ref):
    delta = delta_ref[...]
    tokens, cols = delta.shape
    later = (
        lax.broadcasted_iota(jnp.int32, (tokens, tokens), 1)
        > lax.broadcasted_iota(jnp.int32, (tokens, tokens), 0)
    ).astype(F32)
    after = jnp.dot(
        later, delta, precision=lax.Precision.HIGHEST, preferred_element_type=F32
    )
    total_ref[...] = after[:1] + delta[:1]
    mix = mix_ref[...]
    for n in range(rate_ref.shape[0]):
        fade = jnp.exp(after * -jnp.broadcast_to(rate_ref[n : n + 1], (tokens, cols)))
        reach_ref[n] = (fade * jnp.broadcast_to(mix[:, n : n + 1], (tokens, cols))).astype(BF)


def reach_table(delta, rate, mix):
    tokens, dim = delta.shape
    states = rate.shape[0]
    cols = 512
    return pl.pallas_call(
        reach_body,
        grid=(dim // cols,),
        in_specs=[strip(tokens, cols), strip(states, cols), whole(*mix.shape)],
        out_specs=[
            pl.BlockSpec((states, tokens, cols), lambda i: (0, 0, i)),
            strip(1, cols),
        ],
        out_shape=[
            jax.ShapeDtypeStruct((states, tokens, dim), BF),
            jax.ShapeDtypeStruct((1, dim), F32),
        ],
        compiler_params=params(),
        cost_estimate=pl.CostEstimate(
            flops=8 * states * tokens * dim,
            bytes_accessed=2 * states * tokens * dim,
            transcendentals=states * tokens * dim,
        ),
        name="reach_table",
    )(delta, rate, mix)


def carry_body(place_ref, starts_ref, totals_ref, rate_ref, local_ref, reach_ref, out_ref):
    place = place_ref[0]
    negative = -rate_ref[...]
    tokens, cols = local_ref.shape
    states = negative.shape[0]
    flow = jnp.zeros((states, cols), F32)
    for at in reversed(range(starts_ref.shape[0])):
        passed = jnp.exp(totals_ref[at : at + 1] * negative) * flow
        flow = jnp.where(at > place, starts_ref[at].astype(F32) + passed, flow)
    total = local_ref[...]
    for n in range(states):
        total += reach_ref[n].astype(F32) * flow[n : n + 1]
    out_ref[...] = total.astype(BF)


def add_carry(place, starts, totals, rate, local, reach):
    tokens, dim = local.shape
    states = rate.shape[0]
    blocks = starts.shape[0]
    cols = 256
    return pl.pallas_call(
        carry_body,
        grid=(dim // cols,),
        in_specs=[
            pl.BlockSpec(memory_space=pltpu.SMEM),
            pl.BlockSpec((blocks, states, cols), lambda i: (0, 0, i)),
            strip(blocks, cols),
            strip(states, cols),
            strip(tokens, cols),
            pl.BlockSpec((states, tokens, cols), lambda i: (0, 0, i)),
        ],
        out_specs=strip(tokens, cols),
        out_shape=jax.ShapeDtypeStruct((tokens, dim), BF),
        compiler_params=params(),
        name="add_carry",
    )(place, starts, totals, rate, local, reach)


def on_device(z_size, capacity, x_in, dout, route_ids, combine, w_up, w_down, delta, rate, bmat, cmat):
    x, dy, ids, weights = x_in[0], dout[0], route_ids[0], combine[0]
    up, down, steps = w_up[0], w_down[0], delta[0]

    def shift(value, by):
        ring = [(i, (i + by) % z_size) for i in range(z_size)]
        return lax.ppermute(value, "z", ring)

    def swap(value):
        return lax.ppermute(value, "core", [(0, 1), (1, 0)])

    def across(value, shift_by, sign):
        dx, dy_ = shift_by
        if dx == 0 and dy_ == 0:
            return value
        pairs = [
            (a * SIDE + b, (a + sign * dx) % SIDE * SIDE + (b + sign * dy_) % SIDE)
            for a in range(SIDE)
            for b in range(SIDE)
        ]
        return lax.ppermute(value, "exp", pairs)

    me = lax.axis_index("exp")
    dxs, dys = np.array(SHIFTS, np.int32).T
    order = (me // SIDE + dxs) % SIDE * SIDE + (me % SIDE + dys) % SIDE
    order = order.astype(jnp.int32)

    sent = gather_rows(ids.T, order[:, None], x, dy, capacity)
    got = [across(m, s, 1) for m, s in zip(sent, SHIFTS)]
    quarters = [
        sort_messages(got[i : i + GROUP], capacity) for i in range(0, len(got), GROUP)
    ]
    both = (up, swap(up), down, swap(down))

    def ring(a, b):
        prev_a, next_b = shift(a, 1), shift(b, -1)
        prev_b, next_a = shift(b, 1), shift(a, -1)
        return prev_a, prev_b, next_a, next_b

    def far(prev_a, next_b):
        return shift(prev_a, 1), shift(next_b, -1)

    low_a, low_b, high_a, high_b = quarters
    low = ring(low_a, low_b)
    low_far = far(low[0], low[3])
    reach, total = reach_table(steps, rate, bmat[0])
    low, reach, total = tie(low, reach, total)
    first = expert_rows((low_a, low_b, *low), both)
    high = ring(high_a, high_b)
    low_far, first = tie(low_far, first)
    second = expert_rows((*low_far, high_a, high_b), both)
    high, second = tie(high, second)
    high_far = far(high[0], high[3])
    third = expert_rows(high, both)
    high_far, third = tie(high_far, third)
    fourth = expert_rows(high_far, both)

    def back_home(own, prev, next_, far_a, far_b):
        got_a, got_b = shift(far_a, 1), shift(far_b, -1)
        to_next, to_prev = hop_sums(*next_, *prev, got_a, got_b)
        return pack_returns(*own, shift(to_next, 1), shift(to_prev, -1), capacity)

    backs = [
        *back_home(first[:2], first[2:4], first[4:6], *second[:2]),
        *back_home(second[2:4], third[:2], third[2:4], *fourth),
    ]
    backs = [across(m, s, -1) for m, s in zip(backs, SHIFTS)]

    lanes = (steps.shape[0], bmat.shape[2], 128)
    mix = jnp.broadcast_to(bmat[0][:, :, None], lanes)
    drive = jnp.broadcast_to(cmat[0][:, :, None], lanes)
    totals = lax.all_gather(total[0], ("z", "core"))
    mid, local, start = combine_and_scan(
        ids, order[None, :], weights, backs, dy, steps, rate, mix, drive
    )
    starts = lax.all_gather(start, ("z", "core"))
    place = lax.axis_index(("z", "core")).astype(jnp.int32).reshape(1)
    scan = add_carry(place, starts, totals, rate, local, reach)
    return (mid[None], scan[None])


def solution(mesh):
    seq, exp = mesh.shape["seq"], mesh.shape["exp"]
    z_size = seq // CORES
    split = Mesh(mesh.devices.reshape(z_size, CORES, exp), ("z", "core", "exp"))
    token = P("exp", ("z", "core"), None)

    def run(x_in, dout, route_ids, *rest):
        tokens = route_ids.shape[1] // seq
        capacity = 5 * tokens * route_ids.shape[2] // (4 * exp)
        return jax.shard_map(
            functools.partial(on_device, z_size, capacity),
            mesh=split,
            in_specs=(token,) * 7 + (P(),) + (token,) * 2,
            out_specs=(token, token),
            check_vma=False,
        )(x_in, dout, route_ids, *rest)

    return run
```

```python
import functools

import jax
import jax.numpy as jnp
import numpy as np
from jax import lax
from jax.experimental import pallas as pl
from jax.experimental.pallas import tpu as pltpu
from jax.sharding import Mesh
from jax.sharding import PartitionSpec as P

VMEM_LIMIT = 56 * 1024 * 1024
CORES = 2
EARLY = 12
HIDDEN_STEP = 128
OUT_COLS = 1024
SCAN_COLS = 1024
BF = jnp.bfloat16
F32 = jnp.float32


def params():
    return pltpu.CompilerParams(vmem_limit_bytes=VMEM_LIMIT)


def whole(*shape):
    return pl.BlockSpec(shape, lambda *_: (0,) * len(shape))


def tie(*values):
    return lax.optimization_barrier(values)


def part_sizes(capacity):
    return (EARLY, capacity - EARLY)


def gather_body(capacity, ids_ref, x_ref, dy_ref, *outs):
    tokens = x_ref.shape[0]
    experts = outs[0].shape[0] // (2 * EARLY)
    ids = ids_ref[...]
    at = lax.broadcasted_iota(jnp.int32, (experts, tokens), 0)
    hots = [(at == ids[k : k + 1, :]).astype(F32) for k in range(2)]
    before = (
        lax.broadcasted_iota(jnp.int32, (tokens, tokens), 0)
        < lax.broadcasted_iota(jnp.int32, (tokens, tokens), 1)
    ).astype(F32)
    earlier = jnp.dot(
        (hots[0] + hots[1]).astype(BF), before.astype(BF), preferred_element_type=F32
    )
    slots = [
        jnp.sum(earlier * hot, axis=0, keepdims=True).astype(jnp.int32) for hot in hots
    ]
    first = 0
    for size, out in zip(part_sizes(capacity), outs):
        place = lax.broadcasted_iota(jnp.int32, (out.shape[0], tokens), 0)
        pick_x = pick_dy = None
        for k in range(2):
            slot = slots[k] - first
            inside = (slot >= 0) & (slot < size)
            target = jnp.where(inside, ids[k : k + 1, :] * (2 * size) + slot, -size - 1)
            hit_x, hit_dy = place == target, place == target + size
            pick_x = hit_x if pick_x is None else pick_x | hit_x
            pick_dy = hit_dy if pick_dy is None else pick_dy | hit_dy
        rows = jnp.dot(pick_x.astype(F32).astype(BF), x_ref[...], preferred_element_type=F32)
        rows += jnp.dot(
            pick_dy.astype(F32).astype(BF), dy_ref[...], preferred_element_type=F32
        )
        out[...] = rows.astype(BF)
        first += size


def gather_rows(ids_t, x, dy, experts, capacity):
    dim = x.shape[1]
    return pl.pallas_call(
        functools.partial(gather_body, capacity),
        out_shape=[
            jax.ShapeDtypeStruct((experts * 2 * size, dim), BF)
            for size in part_sizes(capacity)
        ],
        compiler_params=params(),
        name="gather_rows",
    )(ids_t, x, dy)


def sort_body(table_ref, rows_ref, *outs):
    size = outs[0].shape[0]
    for i, out in enumerate(outs):
        rows = rows_ref[i * size : (i + 1) * size]
        out[...] = jnp.dot(table_ref[...], rows, preferred_element_type=F32).astype(BF)


def sort_messages(messages, experts, size):
    count, dim = experts // 2, messages.shape[1]
    rows = 2 * size * count
    at = np.arange(rows)
    kind, rest = at // (size * count), at % (size * count)
    table = np.zeros((rows, rows), np.float32)
    table[at, rest // size * 2 * size + kind * size + rest % size] = 1.0
    return pl.pallas_call(
        sort_body,
        out_shape=[jax.ShapeDtypeStruct((rows, dim), BF)] * 2,
        compiler_params=params(),
        name="sort_messages",
    )(jnp.asarray(table, BF), messages)


def padded(size):
    return -(-size // 8) * 8


def pack_body(spread, *refs):
    if spread:
        table_ref, refs = refs[0], refs[1:]
    own_a, own_b, prev_ref, next_ref, out = refs
    half = own_a.shape[0]
    sums = []
    for own, low in ((own_a, 0), (own_b, half)):
        total = own[...].astype(F32) + prev_ref[low : low + half].astype(F32)
        sums.append((total + next_ref[low : low + half].astype(F32)).astype(BF))
    rows = jnp.concatenate(sums, axis=0)
    if spread:
        rows = jnp.dot(table_ref[...], rows, preferred_element_type=F32).astype(BF)
    out[...] = rows


def pack_returns(own_a, own_b, from_prev, from_next, size):
    rows, dim = from_prev.shape
    wide = padded(size)
    spread = wide != size
    table = np.zeros((rows // size * wide, rows), np.float32)
    at = np.arange(rows)
    table[at // size * wide + at % size, at] = 1.0
    head = (jnp.asarray(table, BF),) if spread else ()
    return pl.pallas_call(
        functools.partial(pack_body, spread),
        out_shape=jax.ShapeDtypeStruct((rows // size * wide, dim), BF),
        compiler_params=params(),
        name="pack_returns",
    )(*head, own_a, own_b, from_prev, from_next)


def hop_body(next_a, next_b, prev_a, prev_b, got_a, got_b, to_next, to_prev):
    half = next_a.shape[0]
    to_next[:half] = (next_a[...].astype(F32) + got_a[...].astype(F32)).astype(BF)
    to_next[half:] = next_b[...]
    to_prev[:half] = prev_a[...]
    to_prev[half:] = (prev_b[...].astype(F32) + got_b[...].astype(F32)).astype(BF)


def hop_sums(*parts):
    half, dim = parts[0].shape
    return pl.pallas_call(
        hop_body,
        out_shape=[jax.ShapeDtypeStruct((2 * half, dim), BF)] * 2,
        compiler_params=params(),
        name="hop_sums",
    )(*parts)


def expert_body(pieces, steps, *refs):
    ins = refs[:pieces]
    up_a, up_b, down_a, down_b = refs[pieces : pieces + 4]
    outs = refs[pieces + 4 : 2 * pieces + 4]
    x_all, dy_all, up_all, grads = refs[2 * pieces + 4 :]
    step = pl.program_id(0)
    width = 2 * up_a.shape[0]

    @pl.when(step == 0)
    def _():
        low = 0
        for piece, out in zip(ins, outs):
            size = out.shape[0]
            x_all[low : low + size] = piece[:size]
            dy_all[low : low + size] = piece[size:]
            low += size

    @pl.when(step < steps)
    def _():
        up = jnp.concatenate([up_a[...], up_b[...]], axis=0)
        down = jnp.concatenate([down_a[...], down_b[...]], axis=0)
        up_all[pl.ds(pl.multiple_of(step * width, width), width)] = up
        across = (((1,), (1,)), ((), ()))
        pre = lax.dot_general(x_all[...], up, across, preferred_element_type=F32)
        back = lax.dot_general(dy_all[...], down, across, preferred_element_type=F32)
        sig = jax.nn.sigmoid(pre)
        grads[step] = (back * sig * (1.0 + pre * (1.0 - sig))).astype(BF)

    @pl.when(step >= steps)
    def _():
        grad = jnp.concatenate([grads[i] for i in range(steps)], axis=1)
        cols = outs[0].shape[1]
        at = pl.ds(pl.multiple_of((step - steps) * cols, cols), cols)
        part = jnp.dot(grad, up_all[:, at], preferred_element_type=F32).astype(BF)
        low = 0
        for out in outs:
            size = out.shape[0]
            out[...] = part[low : low + size]
            low += size


def expert_rows(ins, weights):
    pieces = len(ins)
    dim = ins[0].shape[1]
    sizes = [piece.shape[0] // 2 for piece in ins]
    rows = sum(sizes)
    hidden = weights[0].shape[0]
    steps = hidden // HIDDEN_STEP
    tile = pl.BlockSpec((HIDDEN_STEP, dim), lambda i: (jnp.minimum(i, steps - 1), 0))
    return pl.pallas_call(
        functools.partial(expert_body, pieces, steps),
        grid=(steps + dim // OUT_COLS,),
        in_specs=[whole(*piece.shape) for piece in ins] + [tile] * 4,
        out_specs=[
            pl.BlockSpec((size, OUT_COLS), lambda i: (0, jnp.maximum(i - steps, 0)))
            for size in sizes
        ],
        out_shape=[jax.ShapeDtypeStruct((size, dim), BF) for size in sizes],
        scratch_shapes=[
            pltpu.VMEM((rows, dim), BF),
            pltpu.VMEM((rows, dim), BF),
            pltpu.VMEM((2 * hidden, dim), BF),
            pltpu.VMEM((steps, rows, 2 * HIDDEN_STEP), BF),
        ],
        compiler_params=params(),
        cost_estimate=pl.CostEstimate(
            flops=6 * rows * 2 * hidden * dim,
            bytes_accessed=2 * (4 * hidden * dim + 3 * rows * dim),
            transcendentals=rows * 2 * hidden,
        ),
        name="expert_rows",
    )(*ins, *weights)


def weigh_pair(ids, weights, experts, capacity):
    tokens = ids.shape[0]
    at = lax.broadcasted_iota(jnp.int32, (tokens, experts), 1)
    hots = [(at == ids[:, k : k + 1]).astype(F32) for k in range(2)]
    before = (
        lax.broadcasted_iota(jnp.int32, (tokens, tokens), 1)
        < lax.broadcasted_iota(jnp.int32, (tokens, tokens), 0)
    ).astype(F32)
    earlier = jnp.dot(
        before.astype(BF), (hots[0] + hots[1]).astype(BF), preferred_element_type=F32
    )
    sizes = part_sizes(capacity)
    rows = experts * sum(padded(size) for size in sizes)
    place = lax.broadcasted_iota(jnp.int32, (tokens, rows), 1)
    table = jnp.zeros((tokens, rows), F32)
    for k in range(2):
        slot = jnp.sum(earlier * hots[k], axis=1, keepdims=True).astype(jnp.int32)
        own = ids[:, k : k + 1]
        target = jnp.where(
            slot < sizes[0],
            own * padded(sizes[0]) + slot,
            experts * padded(sizes[0]) + own * padded(sizes[1]) + slot - sizes[0],
        )
        table = table + jnp.where(place == target, weights[:, k : k + 1], 0.0)
    high = table.astype(BF)
    low = (table - high.astype(F32)).astype(BF)
    return high, low


def scan_body(experts, capacity, ids_ref, weights_ref, *refs):
    backs = refs[:2]
    dout_ref, delta_ref, rate_ref, mix_ref, drive_ref = refs[2:7]
    mid_ref, local_ref, start_ref, grad = refs[7:]
    high, low = weigh_pair(ids_ref[...], weights_ref[...], experts, capacity)
    back = jnp.concatenate([b[...] for b in backs], axis=0)
    routed = jnp.dot(high, back, preferred_element_type=F32)
    routed += jnp.dot(low, back, preferred_element_type=F32)
    mid = (dout_ref[...].astype(F32) + routed).astype(BF)
    mid_ref[...] = mid
    grad[...] = mid.astype(F32)
    negative = -rate_ref[...]
    tokens, cols = grad.shape
    states = negative.shape[0]
    repeat = cols // mix_ref.shape[2]

    def block(i, flow):
        low_t = pl.multiple_of((tokens // 8 - 1 - i) * 8, 8)
        grads = grad[pl.ds(low_t, 8)]
        deltas = delta_ref[pl.ds(low_t, 8)]
        rows = []
        for r in reversed(range(8)):
            drive = jnp.concatenate([drive_ref[low_t + r]] * repeat, axis=1)
            mix = jnp.concatenate([mix_ref[low_t + r]] * repeat, axis=1)
            state = drive * jnp.broadcast_to(grads[r : r + 1], (states, cols)) + flow
            rows.append(jnp.sum(mix * state, axis=0, keepdims=True))
            decay = jnp.exp(jnp.broadcast_to(deltas[r : r + 1], (states, cols)) * negative)
            flow = decay * state
        local_ref[pl.ds(low_t, 8)] = jnp.concatenate(rows[::-1], axis=0)
        return flow

    start_ref[...] = lax.fori_loop(
        0, tokens // 8, block, jnp.zeros((states, cols), F32)
    ).astype(BF)


def strip(rows, cols):
    return pl.BlockSpec((rows, cols), lambda i: (0, i))


def combine_and_scan(ids, weights, backs, dout, delta, rate, mix, drive, experts, capacity):
    tokens, dim = dout.shape
    states = rate.shape[0]
    cols = SCAN_COLS
    return pl.pallas_call(
        functools.partial(scan_body, experts, capacity),
        grid=(dim // cols,),
        in_specs=[whole(*ids.shape), whole(*weights.shape)]
        + [strip(b.shape[0], cols) for b in backs]
        + [
            strip(tokens, cols),
            strip(tokens, cols),
            strip(states, cols),
            whole(*mix.shape),
            whole(*drive.shape),
        ],
        out_specs=[strip(tokens, cols), strip(tokens, cols), strip(states, cols)],
        out_shape=[
            jax.ShapeDtypeStruct((tokens, dim), BF),
            jax.ShapeDtypeStruct((tokens, dim), F32),
            jax.ShapeDtypeStruct((states, dim), BF),
        ],
        scratch_shapes=[pltpu.VMEM((tokens, cols), F32)],
        compiler_params=params(),
        name="combine_and_scan",
    )(ids, weights, *backs, dout, delta, rate, mix, drive)


def reach_body(delta_ref, rate_ref, mix_ref, reach_ref, total_ref):
    delta = delta_ref[...]
    tokens, cols = delta.shape
    later = (
        lax.broadcasted_iota(jnp.int32, (tokens, tokens), 1)
        > lax.broadcasted_iota(jnp.int32, (tokens, tokens), 0)
    ).astype(F32)
    after = jnp.dot(
        later, delta, precision=lax.Precision.HIGHEST, preferred_element_type=F32
    )
    total_ref[...] = after[:1] + delta[:1]
    mix = mix_ref[...]
    for n in range(rate_ref.shape[0]):
        fade = jnp.exp(after * -jnp.broadcast_to(rate_ref[n : n + 1], (tokens, cols)))
        reach_ref[n] = (fade * jnp.broadcast_to(mix[:, n : n + 1], (tokens, cols))).astype(BF)


def reach_table(delta, rate, mix):
    tokens, dim = delta.shape
    states = rate.shape[0]
    cols = 512
    return pl.pallas_call(
        reach_body,
        grid=(dim // cols,),
        in_specs=[strip(tokens, cols), strip(states, cols), whole(*mix.shape)],
        out_specs=[
            pl.BlockSpec((states, tokens, cols), lambda i: (0, 0, i)),
            strip(1, cols),
        ],
        out_shape=[
            jax.ShapeDtypeStruct((states, tokens, dim), BF),
            jax.ShapeDtypeStruct((1, dim), F32),
        ],
        compiler_params=params(),
        cost_estimate=pl.CostEstimate(
            flops=8 * states * tokens * dim,
            bytes_accessed=2 * states * tokens * dim,
            transcendentals=states * tokens * dim,
        ),
        name="reach_table",
    )(delta, rate, mix)


def carry_body(place_ref, starts_ref, totals_ref, rate_ref, local_ref, reach_ref, out_ref):
    place = place_ref[0]
    negative = -rate_ref[...]
    tokens, cols = local_ref.shape
    states = negative.shape[0]
    flow = jnp.zeros((states, cols), F32)
    for at in reversed(range(starts_ref.shape[0])):
        passed = jnp.exp(totals_ref[at : at + 1] * negative) * flow
        flow = jnp.where(at > place, starts_ref[at].astype(F32) + passed, flow)
    total = local_ref[...]
    for n in range(states):
        total += reach_ref[n].astype(F32) * flow[n : n + 1]
    out_ref[...] = total.astype(BF)


def add_carry(place, starts, totals, rate, local, reach):
    tokens, dim = local.shape
    states = rate.shape[0]
    blocks = starts.shape[0]
    cols = SCAN_COLS
    return pl.pallas_call(
        carry_body,
        grid=(dim // cols,),
        in_specs=[
            pl.BlockSpec(memory_space=pltpu.SMEM),
            pl.BlockSpec((blocks, states, cols), lambda i: (0, 0, i)),
            strip(blocks, cols),
            strip(states, cols),
            strip(tokens, cols),
            pl.BlockSpec((states, tokens, cols), lambda i: (0, 0, i)),
        ],
        out_specs=strip(tokens, cols),
        out_shape=jax.ShapeDtypeStruct((tokens, dim), BF),
        compiler_params=params(),
        name="add_carry",
    )(place, starts, totals, rate, local, reach)


def on_device(z_size, capacity, x_in, dout, route_ids, combine, w_up, w_down, delta, rate, bmat, cmat):
    experts = lax.axis_size("exp")
    x, dy, ids, weights = x_in[0], dout[0], route_ids[0], combine[0]
    up, down, steps = w_up[0], w_down[0], delta[0]

    def shift(value, by):
        ring = [(i, (i + by) % z_size) for i in range(z_size)]
        return lax.ppermute(value, "z", ring)

    def swap(value):
        return lax.ppermute(value, "core", [(0, 1), (1, 0)])

    def exchange(value):
        parts = value.reshape(experts, -1, value.shape[1])
        got = lax.all_to_all(parts, "exp", split_axis=0, concat_axis=0, tiled=True)
        return got.reshape(value.shape)

    sizes = part_sizes(capacity)
    sent = gather_rows(ids.T, x, dy, experts, capacity)
    up_other, down_other = swap(up), swap(down)
    got_low = exchange(sent[0])
    got_low, up_other, down_other = tie(got_low, up_other, down_other)
    both = (up, up_other, down, down_other)
    low_a, low_b = sort_messages(got_low, experts, sizes[0])
    high_a, high_b = sort_messages(exchange(sent[1]), experts, sizes[1])

    def ring(a, b):
        prev_a, next_b = shift(a, 1), shift(b, -1)
        prev_b, next_a = shift(b, 1), shift(a, -1)
        return prev_a, prev_b, next_a, next_b

    def far(prev_a, next_b):
        return shift(prev_a, 1), shift(next_b, -1)

    low = ring(low_a, low_b)
    low_far = far(low[0], low[3])
    lanes = (steps.shape[0], bmat.shape[2], 128)
    mix = jnp.broadcast_to(bmat[0][:, :, None], lanes)
    drive = jnp.broadcast_to(cmat[0][:, :, None], lanes)
    reach, total = reach_table(steps, rate, bmat[0])
    totals = lax.all_gather(total[0], ("z", "core"))
    low, reach, totals, mix, drive = tie(low, reach, totals, mix, drive)
    first = expert_rows((low_a, low_b, *low), both)
    high = ring(high_a, high_b)
    low_far, first = tie(low_far, first)
    second = expert_rows((*low_far, high_a, high_b), both)
    high, second = tie(high, second)
    high_far = far(high[0], high[3])
    third = expert_rows(high, both)
    low_sums = hop_sums(*first[4:6], *first[2:4], shift(second[0], 1), shift(second[1], -1))
    high_far, third, low_sums = tie(high_far, third, low_sums)
    fourth = expert_rows(high_far, both)

    def home(own, sums, size):
        to_next, to_prev = sums
        return pack_returns(*own, shift(to_next, 1), shift(to_prev, -1), size)

    low_home = home(first[:2], low_sums, sizes[0])
    high_got = (shift(fourth[0], 1), shift(fourth[1], -1))
    low_home, high_got = tie(low_home, high_got)
    low_back = exchange(low_home)
    high_sums = hop_sums(*third[2:4], *third[:2], *high_got)
    backs = (low_back, exchange(home(second[2:4], high_sums, sizes[1])))

    mid, local, start = combine_and_scan(
        ids, weights, backs, dy, steps, rate, mix, drive, experts, capacity
    )
    starts = lax.all_gather(start, ("z", "core"))
    place = lax.axis_index(("z", "core")).astype(jnp.int32).reshape(1)
    scan = add_carry(place, starts, totals, rate, local, reach)
    return (mid[None], scan[None])


def solution(mesh):
    seq, exp = mesh.shape["seq"], mesh.shape["exp"]
    z_size = seq // CORES
    split = Mesh(mesh.devices.reshape(z_size, CORES, exp), ("z", "core", "exp"))
    token = P("exp", ("z", "core"), None)

    def run(x_in, dout, route_ids, *rest):
        tokens = route_ids.shape[1] // seq
        capacity = 5 * tokens * route_ids.shape[2] // (4 * exp)
        return jax.shard_map(
            functools.partial(on_device, z_size, capacity),
            mesh=split,
            in_specs=(token,) * 7 + (P(),) + (token,) * 2,
            out_specs=(token, token),
            check_vma=False,
        )(x_in, dout, route_ids, *rest)

    return run
```

```python
import functools

import jax
import jax.numpy as jnp
import numpy as np
from jax import lax
from jax.experimental import pallas as pl
from jax.experimental.pallas import tpu as pltpu
from jax.sharding import Mesh
from jax.sharding import PartitionSpec as P

VMEM_LIMIT = 56 * 1024 * 1024
CORES = 2
EARLY = 12
HIDDEN_STEP = 128
OUT_COLS = 1024
SCAN_COLS = 1024
BF = jnp.bfloat16
F32 = jnp.float32


def params():
    return pltpu.CompilerParams(vmem_limit_bytes=VMEM_LIMIT)


def whole(*shape):
    return pl.BlockSpec(shape, lambda *_: (0,) * len(shape))


def tie(*values):
    return lax.optimization_barrier(values)


def part_sizes(capacity):
    return (EARLY, capacity - EARLY)


def gather_body(capacity, ids_ref, x_ref, dy_ref, *outs):
    tokens = x_ref.shape[0]
    experts = outs[0].shape[0] // (2 * EARLY)
    ids = ids_ref[...]
    at = lax.broadcasted_iota(jnp.int32, (experts, tokens), 0)
    hots = [(at == ids[k : k + 1, :]).astype(F32) for k in range(2)]
    before = (
        lax.broadcasted_iota(jnp.int32, (tokens, tokens), 0)
        < lax.broadcasted_iota(jnp.int32, (tokens, tokens), 1)
    ).astype(F32)
    earlier = jnp.dot(
        (hots[0] + hots[1]).astype(BF), before.astype(BF), preferred_element_type=F32
    )
    slots = [
        jnp.sum(earlier * hot, axis=0, keepdims=True).astype(jnp.int32) for hot in hots
    ]
    first = 0
    for size, out in zip(part_sizes(capacity), outs):
        place = lax.broadcasted_iota(jnp.int32, (out.shape[0], tokens), 0)
        pick_x = pick_dy = None
        for k in range(2):
            slot = slots[k] - first
            inside = (slot >= 0) & (slot < size)
            target = jnp.where(inside, ids[k : k + 1, :] * (2 * size) + slot, -size - 1)
            hit_x, hit_dy = place == target, place == target + size
            pick_x = hit_x if pick_x is None else pick_x | hit_x
            pick_dy = hit_dy if pick_dy is None else pick_dy | hit_dy
        rows = jnp.dot(pick_x.astype(F32).astype(BF), x_ref[...], preferred_element_type=F32)
        rows += jnp.dot(
            pick_dy.astype(F32).astype(BF), dy_ref[...], preferred_element_type=F32
        )
        out[...] = rows.astype(BF)
        first += size


def gather_rows(ids_t, x, dy, experts, capacity):
    dim = x.shape[1]
    return pl.pallas_call(
        functools.partial(gather_body, capacity),
        out_shape=[
            jax.ShapeDtypeStruct((experts * 2 * size, dim), BF)
            for size in part_sizes(capacity)
        ],
        compiler_params=params(),
        name="gather_rows",
    )(ids_t, x, dy)


def sort_body(table_ref, rows_ref, *outs):
    size = outs[0].shape[0]
    for i, out in enumerate(outs):
        rows = rows_ref[i * size : (i + 1) * size]
        out[...] = jnp.dot(table_ref[...], rows, preferred_element_type=F32).astype(BF)


def sort_messages(messages, experts, size):
    count, dim = experts // 2, messages.shape[1]
    rows = 2 * size * count
    at = np.arange(rows)
    kind, rest = at // (size * count), at % (size * count)
    table = np.zeros((rows, rows), np.float32)
    table[at, rest // size * 2 * size + kind * size + rest % size] = 1.0
    return pl.pallas_call(
        sort_body,
        out_shape=[jax.ShapeDtypeStruct((rows, dim), BF)] * 2,
        compiler_params=params(),
        name="sort_messages",
    )(jnp.asarray(table, BF), messages)


def padded(size):
    return -(-size // 8) * 8


def pack_body(spread, *refs):
    if spread:
        table_ref, refs = refs[0], refs[1:]
    own_a, own_b, prev_ref, next_ref, out = refs
    half = own_a.shape[0]
    sums = []
    for own, low in ((own_a, 0), (own_b, half)):
        total = own[...].astype(F32) + prev_ref[low : low + half].astype(F32)
        sums.append((total + next_ref[low : low + half].astype(F32)).astype(BF))
    rows = jnp.concatenate(sums, axis=0)
    if spread:
        rows = jnp.dot(table_ref[...], rows, preferred_element_type=F32).astype(BF)
    out[...] = rows


def pack_returns(own_a, own_b, from_prev, from_next, size):
    rows, dim = from_prev.shape
    wide = padded(size)
    spread = wide != size
    table = np.zeros((rows // size * wide, rows), np.float32)
    at = np.arange(rows)
    table[at // size * wide + at % size, at] = 1.0
    head = (jnp.asarray(table, BF),) if spread else ()
    return pl.pallas_call(
        functools.partial(pack_body, spread),
        out_shape=jax.ShapeDtypeStruct((rows // size * wide, dim), BF),
        compiler_params=params(),
        name="pack_returns",
    )(*head, own_a, own_b, from_prev, from_next)


def hop_body(next_a, next_b, prev_a, prev_b, got_a, got_b, to_next, to_prev):
    half = next_a.shape[0]
    to_next[:half] = (next_a[...].astype(F32) + got_a[...].astype(F32)).astype(BF)
    to_next[half:] = next_b[...]
    to_prev[:half] = prev_a[...]
    to_prev[half:] = (prev_b[...].astype(F32) + got_b[...].astype(F32)).astype(BF)


def hop_sums(*parts):
    half, dim = parts[0].shape
    return pl.pallas_call(
        hop_body,
        out_shape=[jax.ShapeDtypeStruct((2 * half, dim), BF)] * 2,
        compiler_params=params(),
        name="hop_sums",
    )(*parts)


def expert_body(pieces, steps, *refs):
    ins = refs[:pieces]
    up_a, up_b, down_a, down_b = refs[pieces : pieces + 4]
    outs = refs[pieces + 4 : 2 * pieces + 4]
    x_all, dy_all, up_all, grads = refs[2 * pieces + 4 :]
    step = pl.program_id(0)
    width = 2 * up_a.shape[0]

    @pl.when(step == 0)
    def _():
        low = 0
        for piece, out in zip(ins, outs):
            size = out.shape[0]
            x_all[low : low + size] = piece[:size]
            dy_all[low : low + size] = piece[size:]
            low += size

    @pl.when(step < steps)
    def _():
        up = jnp.concatenate([up_a[...], up_b[...]], axis=0)
        down = jnp.concatenate([down_a[...], down_b[...]], axis=0)
        up_all[pl.ds(pl.multiple_of(step * width, width), width)] = up
        across = (((1,), (1,)), ((), ()))
        pre = lax.dot_general(x_all[...], up, across, preferred_element_type=F32)
        back = lax.dot_general(dy_all[...], down, across, preferred_element_type=F32)
        sig = jax.nn.sigmoid(pre)
        grads[step] = (back * sig * (1.0 + pre * (1.0 - sig))).astype(BF)

    @pl.when(step >= steps)
    def _():
        grad = jnp.concatenate([grads[i] for i in range(steps)], axis=1)
        cols = outs[0].shape[1]
        at = pl.ds(pl.multiple_of((step - steps) * cols, cols), cols)
        part = jnp.dot(grad, up_all[:, at], preferred_element_type=F32).astype(BF)
        low = 0
        for out in outs:
            size = out.shape[0]
            out[...] = part[low : low + size]
            low += size


def expert_rows(ins, weights):
    pieces = len(ins)
    dim = ins[0].shape[1]
    sizes = [piece.shape[0] // 2 for piece in ins]
    rows = sum(sizes)
    hidden = weights[0].shape[0]
    steps = hidden // HIDDEN_STEP
    tile = pl.BlockSpec((HIDDEN_STEP, dim), lambda i: (jnp.minimum(i, steps - 1), 0))
    return pl.pallas_call(
        functools.partial(expert_body, pieces, steps),
        grid=(steps + dim // OUT_COLS,),
        in_specs=[whole(*piece.shape) for piece in ins] + [tile] * 4,
        out_specs=[
            pl.BlockSpec((size, OUT_COLS), lambda i: (0, jnp.maximum(i - steps, 0)))
            for size in sizes
        ],
        out_shape=[jax.ShapeDtypeStruct((size, dim), BF) for size in sizes],
        scratch_shapes=[
            pltpu.VMEM((rows, dim), BF),
            pltpu.VMEM((rows, dim), BF),
            pltpu.VMEM((2 * hidden, dim), BF),
            pltpu.VMEM((steps, rows, 2 * HIDDEN_STEP), BF),
        ],
        compiler_params=params(),
        cost_estimate=pl.CostEstimate(
            flops=6 * rows * 2 * hidden * dim,
            bytes_accessed=2 * (4 * hidden * dim + 3 * rows * dim),
            transcendentals=rows * 2 * hidden,
        ),
        name="expert_rows",
    )(*ins, *weights)


def weigh_pair(ids, weights, experts, capacity):
    tokens = ids.shape[0]
    at = lax.broadcasted_iota(jnp.int32, (tokens, experts), 1)
    hots = [(at == ids[:, k : k + 1]).astype(F32) for k in range(2)]
    before = (
        lax.broadcasted_iota(jnp.int32, (tokens, tokens), 1)
        < lax.broadcasted_iota(jnp.int32, (tokens, tokens), 0)
    ).astype(F32)
    earlier = jnp.dot(
        before.astype(BF), (hots[0] + hots[1]).astype(BF), preferred_element_type=F32
    )
    sizes = part_sizes(capacity)
    rows = experts * sum(padded(size) for size in sizes)
    place = lax.broadcasted_iota(jnp.int32, (tokens, rows), 1)
    table = jnp.zeros((tokens, rows), F32)
    for k in range(2):
        slot = jnp.sum(earlier * hots[k], axis=1, keepdims=True).astype(jnp.int32)
        own = ids[:, k : k + 1]
        target = jnp.where(
            slot < sizes[0],
            own * padded(sizes[0]) + slot,
            experts * padded(sizes[0]) + own * padded(sizes[1]) + slot - sizes[0],
        )
        table = table + jnp.where(place == target, weights[:, k : k + 1], 0.0)
    high = table.astype(BF)
    low = (table - high.astype(F32)).astype(BF)
    return high, low


def table_body(experts, capacity, ids_ref, weights_ref, high_ref, low_ref):
    high_ref[...], low_ref[...] = weigh_pair(
        ids_ref[...], weights_ref[...], experts, capacity
    )


def weigh_tables(ids, weights, experts, capacity):
    rows = experts * sum(padded(size) for size in part_sizes(capacity))
    return pl.pallas_call(
        functools.partial(table_body, experts, capacity),
        out_shape=[jax.ShapeDtypeStruct((ids.shape[0], rows), BF)] * 2,
        compiler_params=params(),
        name="weigh_tables",
    )(ids, weights)


def scan_body(*refs):
    high_ref, low_ref = refs[:2]
    backs = refs[2:4]
    dout_ref, delta_ref, rate_ref, total_ref, mix_ref, drive_ref = refs[4:10]
    mid_ref, local_ref, start_ref, grad = refs[10:]
    back = jnp.concatenate([b[...] for b in backs], axis=0)
    routed = jnp.dot(high_ref[...], back, preferred_element_type=F32)
    routed += jnp.dot(low_ref[...], back, preferred_element_type=F32)
    mid = (dout_ref[...].astype(F32) + routed).astype(BF)
    mid_ref[...] = mid
    grad[...] = mid.astype(F32)
    negative = -rate_ref[...]
    tokens, cols = grad.shape
    states = negative.shape[0]
    repeat = cols // mix_ref.shape[2]

    def block(i, flow):
        low_t = pl.multiple_of((tokens // 8 - 1 - i) * 8, 8)
        grads = grad[pl.ds(low_t, 8)]
        deltas = delta_ref[pl.ds(low_t, 8)]
        rows = []
        for r in reversed(range(8)):
            drive = jnp.concatenate([drive_ref[low_t + r]] * repeat, axis=1)
            mix = jnp.concatenate([mix_ref[low_t + r]] * repeat, axis=1)
            state = drive * jnp.broadcast_to(grads[r : r + 1], (states, cols)) + flow
            rows.append(jnp.sum(mix * state, axis=0, keepdims=True))
            decay = jnp.exp(jnp.broadcast_to(deltas[r : r + 1], (states, cols)) * negative)
            flow = decay * state
        local_ref[pl.ds(low_t, 8)] = jnp.concatenate(rows[::-1], axis=0)
        return flow

    flow = lax.fori_loop(0, tokens // 8, block, jnp.zeros((states, cols), F32))
    total = jnp.broadcast_to(total_ref[...], (8, cols))
    whole_part = total.astype(BF).astype(F32)
    row = lax.broadcasted_iota(jnp.int32, (8, cols), 0)
    tail = jnp.where(row == 0, whole_part, jnp.where(row == 1, total - whole_part, 0.0))
    start_ref[...] = jnp.concatenate([flow, tail], axis=0).astype(BF)


def strip(rows, cols):
    return pl.BlockSpec((rows, cols), lambda i: (0, i))


def combine_and_scan(tables, backs, dout, delta, rate, total, mix, drive):
    tokens, dim = dout.shape
    states = rate.shape[0]
    cols = SCAN_COLS
    return pl.pallas_call(
        scan_body,
        grid=(dim // cols,),
        in_specs=[whole(*t.shape) for t in tables]
        + [strip(b.shape[0], cols) for b in backs]
        + [
            strip(tokens, cols),
            strip(tokens, cols),
            strip(states, cols),
            strip(1, cols),
            whole(*mix.shape),
            whole(*drive.shape),
        ],
        out_specs=[strip(tokens, cols), strip(tokens, cols), strip(states + 8, cols)],
        out_shape=[
            jax.ShapeDtypeStruct((tokens, dim), BF),
            jax.ShapeDtypeStruct((tokens, dim), F32),
            jax.ShapeDtypeStruct((states + 8, dim), BF),
        ],
        scratch_shapes=[pltpu.VMEM((tokens, cols), F32)],
        compiler_params=params(),
        name="combine_and_scan",
    )(*tables, *backs, dout, delta, rate, total, mix, drive)


def reach_body(delta_ref, rate_ref, mix_ref, reach_ref, total_ref):
    delta = delta_ref[...]
    tokens, cols = delta.shape
    later = (
        lax.broadcasted_iota(jnp.int32, (tokens, tokens), 1)
        > lax.broadcasted_iota(jnp.int32, (tokens, tokens), 0)
    ).astype(F32)
    after = jnp.dot(
        later, delta, precision=lax.Precision.HIGHEST, preferred_element_type=F32
    )
    total_ref[...] = after[:1] + delta[:1]
    mix = mix_ref[...]
    for n in range(rate_ref.shape[0]):
        fade = jnp.exp(after * -jnp.broadcast_to(rate_ref[n : n + 1], (tokens, cols)))
        reach_ref[n] = (fade * jnp.broadcast_to(mix[:, n : n + 1], (tokens, cols))).astype(BF)


def reach_table(delta, rate, mix):
    tokens, dim = delta.shape
    states = rate.shape[0]
    cols = 512
    return pl.pallas_call(
        reach_body,
        grid=(dim // cols,),
        in_specs=[strip(tokens, cols), strip(states, cols), whole(*mix.shape)],
        out_specs=[
            pl.BlockSpec((states, tokens, cols), lambda i: (0, 0, i)),
            strip(1, cols),
        ],
        out_shape=[
            jax.ShapeDtypeStruct((states, tokens, dim), BF),
            jax.ShapeDtypeStruct((1, dim), F32),
        ],
        compiler_params=params(),
        cost_estimate=pl.CostEstimate(
            flops=8 * states * tokens * dim,
            bytes_accessed=2 * states * tokens * dim,
            transcendentals=states * tokens * dim,
        ),
        name="reach_table",
    )(delta, rate, mix)


def carry_body(place_ref, starts_ref, rate_ref, local_ref, reach_ref, out_ref):
    place = place_ref[0]
    negative = -rate_ref[...]
    tokens, cols = local_ref.shape
    states = negative.shape[0]
    flow = jnp.zeros((states, cols), F32)
    for at in reversed(range(starts_ref.shape[0])):
        sent = starts_ref[at].astype(F32)
        total = sent[states : states + 1] + sent[states + 1 : states + 2]
        passed = jnp.exp(total * negative) * flow
        flow = jnp.where(at > place, sent[:states] + passed, flow)
    total = local_ref[...]
    for n in range(states):
        total += reach_ref[n].astype(F32) * flow[n : n + 1]
    out_ref[...] = total.astype(BF)


def add_carry(place, starts, rate, local, reach):
    tokens, dim = local.shape
    states = rate.shape[0]
    blocks = starts.shape[0]
    cols = SCAN_COLS
    return pl.pallas_call(
        carry_body,
        grid=(dim // cols,),
        in_specs=[
            pl.BlockSpec(memory_space=pltpu.SMEM),
            pl.BlockSpec((blocks, states + 8, cols), lambda i: (0, 0, i)),
            strip(states, cols),
            strip(tokens, cols),
            pl.BlockSpec((states, tokens, cols), lambda i: (0, 0, i)),
        ],
        out_specs=strip(tokens, cols),
        out_shape=jax.ShapeDtypeStruct((tokens, dim), BF),
        compiler_params=params(),
        name="add_carry",
    )(place, starts, rate, local, reach)


def on_device(z_size, capacity, x_in, dout, route_ids, combine, w_up, w_down, delta, rate, bmat, cmat):
    experts = lax.axis_size("exp")
    x, dy, ids, weights = x_in[0], dout[0], route_ids[0], combine[0]
    up, down, steps = w_up[0], w_down[0], delta[0]

    def shift(value, by):
        ring = [(i, (i + by) % z_size) for i in range(z_size)]
        return lax.ppermute(value, "z", ring)

    def swap(value):
        return lax.ppermute(value, "core", [(0, 1), (1, 0)])

    def exchange(value):
        parts = value.reshape(experts, -1, value.shape[1])
        got = lax.all_to_all(parts, "exp", split_axis=0, concat_axis=0, tiled=True)
        return got.reshape(value.shape)

    sizes = part_sizes(capacity)
    sent = gather_rows(ids.T, x, dy, experts, capacity)
    up_other, down_other = swap(up), swap(down)
    got_low = exchange(sent[0])
    got_low, up_other, down_other = tie(got_low, up_other, down_other)
    both = (up, up_other, down, down_other)
    low_a, low_b = sort_messages(got_low, experts, sizes[0])
    high_a, high_b = sort_messages(exchange(sent[1]), experts, sizes[1])

    def ring(a, b):
        prev_a, next_b = shift(a, 1), shift(b, -1)
        prev_b, next_a = shift(b, 1), shift(a, -1)
        return prev_a, prev_b, next_a, next_b

    def far(prev_a, next_b):
        return shift(prev_a, 1), shift(next_b, -1)

    low = ring(low_a, low_b)
    low_far = far(low[0], low[3])
    lanes = (steps.shape[0], bmat.shape[2], 128)
    mix = jnp.broadcast_to(bmat[0][:, :, None], lanes)
    drive = jnp.broadcast_to(cmat[0][:, :, None], lanes)
    reach, total = reach_table(steps, rate, bmat[0])
    tables = weigh_tables(ids, weights, experts, capacity)
    low, reach, total, tables, mix, drive = tie(low, reach, total, tables, mix, drive)
    first = expert_rows((low_a, low_b, *low), both)
    high = ring(high_a, high_b)
    low_far, first = tie(low_far, first)
    second = expert_rows((*low_far, high_a, high_b), both)
    high, second = tie(high, second)
    high_far = far(high[0], high[3])
    third = expert_rows(high, both)
    low_sums = hop_sums(*first[4:6], *first[2:4], shift(second[0], 1), shift(second[1], -1))
    high_far, third, low_sums = tie(high_far, third, low_sums)
    fourth = expert_rows(high_far, both)

    def home(own, sums, size):
        to_next, to_prev = sums
        return pack_returns(*own, shift(to_next, 1), shift(to_prev, -1), size)

    low_home = home(first[:2], low_sums, sizes[0])
    high_got = (shift(fourth[0], 1), shift(fourth[1], -1))
    low_home, high_got = tie(low_home, high_got)
    low_back = exchange(low_home)
    high_sums = hop_sums(*third[2:4], *third[:2], *high_got)
    backs = (low_back, exchange(home(second[2:4], high_sums, sizes[1])))

    mid, local, start = combine_and_scan(
        tables, backs, dy, steps, rate, total, mix, drive
    )
    starts = lax.all_gather(start, ("z", "core"))
    place = lax.axis_index(("z", "core")).astype(jnp.int32).reshape(1)
    scan = add_carry(place, starts, rate, local, reach)
    return (mid[None], scan[None])


def solution(mesh):
    seq, exp = mesh.shape["seq"], mesh.shape["exp"]
    z_size = seq // CORES
    split = Mesh(mesh.devices.reshape(z_size, CORES, exp), ("z", "core", "exp"))
    token = P("exp", ("z", "core"), None)

    def run(x_in, dout, route_ids, *rest):
        tokens = route_ids.shape[1] // seq
        capacity = 5 * tokens * route_ids.shape[2] // (4 * exp)
        return jax.shard_map(
            functools.partial(on_device, z_size, capacity),
            mesh=split,
            in_specs=(token,) * 7 + (P(),) + (token,) * 2,
            out_specs=(token, token),
            check_vma=False,
        )(x_in, dout, route_ids, *rest)

    return run
```

```python
import functools

import jax
import jax.numpy as jnp
import numpy as np
from jax import lax
from jax.experimental import pallas as pl
from jax.experimental.pallas import tpu as pltpu
from jax.sharding import Mesh
from jax.sharding import PartitionSpec as P

CORES = 2
EARLY = 12
HIDDEN_STEP = 128
OUT_COLS = 512
SCAN_COLS = 1024
BF = jnp.bfloat16
F32 = jnp.float32


def params(mebibytes):
    return pltpu.CompilerParams(vmem_limit_bytes=mebibytes * 1024 * 1024)


def in_vmem(values):
    return [pltpu.with_memory_space_constraint(v, pltpu.VMEM) for v in values]


def whole(*shape):
    return pl.BlockSpec(shape, lambda *_: (0,) * len(shape))


def tie(*values):
    return lax.optimization_barrier(values)


def part_sizes(capacity):
    return (EARLY, capacity - EARLY)


def gather_body(capacity, ids_ref, x_ref, dy_ref, *outs):
    tokens = x_ref.shape[0]
    experts = outs[0].shape[0] // (2 * EARLY)
    ids = ids_ref[...]
    at = lax.broadcasted_iota(jnp.int32, (experts, tokens), 0)
    hots = [(at == ids[k : k + 1, :]).astype(F32) for k in range(2)]
    before = (
        lax.broadcasted_iota(jnp.int32, (tokens, tokens), 0)
        < lax.broadcasted_iota(jnp.int32, (tokens, tokens), 1)
    ).astype(F32)
    earlier = jnp.dot(
        (hots[0] + hots[1]).astype(BF), before.astype(BF), preferred_element_type=F32
    )
    slots = [
        jnp.sum(earlier * hot, axis=0, keepdims=True).astype(jnp.int32) for hot in hots
    ]
    first = 0
    for size, out in zip(part_sizes(capacity), outs):
        place = lax.broadcasted_iota(jnp.int32, (out.shape[0], tokens), 0)
        pick_x = pick_dy = None
        for k in range(2):
            slot = slots[k] - first
            inside = (slot >= 0) & (slot < size)
            target = jnp.where(inside, ids[k : k + 1, :] * (2 * size) + slot, -size - 1)
            hit_x, hit_dy = place == target, place == target + size
            pick_x = hit_x if pick_x is None else pick_x | hit_x
            pick_dy = hit_dy if pick_dy is None else pick_dy | hit_dy
        rows = jnp.dot(pick_x.astype(F32).astype(BF), x_ref[...], preferred_element_type=F32)
        rows += jnp.dot(
            pick_dy.astype(F32).astype(BF), dy_ref[...], preferred_element_type=F32
        )
        out[...] = rows.astype(BF)
        first += size


def gather_rows(ids_t, x, dy, experts, capacity):
    dim = x.shape[1]
    return pl.pallas_call(
        functools.partial(gather_body, capacity),
        out_shape=[
            jax.ShapeDtypeStruct((experts * 2 * size, dim), BF)
            for size in part_sizes(capacity)
        ],
        compiler_params=params(40),
        name="gather_rows",
    )(ids_t, x, dy)


def sort_body(table_ref, rows_ref, *outs):
    size = outs[0].shape[0]
    for i, out in enumerate(outs):
        rows = rows_ref[i * size : (i + 1) * size]
        out[...] = jnp.dot(table_ref[...], rows, preferred_element_type=F32).astype(BF)


def sort_messages(messages, experts, size):
    count, dim = experts // 2, messages.shape[1]
    rows = 2 * size * count
    at = np.arange(rows)
    kind, rest = at // (size * count), at % (size * count)
    table = np.zeros((rows, rows), np.float32)
    table[at, rest // size * 2 * size + kind * size + rest % size] = 1.0
    return pl.pallas_call(
        sort_body,
        out_shape=[jax.ShapeDtypeStruct((rows, dim), BF)] * 2,
        compiler_params=params(38),
        name="sort_messages",
    )(jnp.asarray(table, BF), *in_vmem((messages,)))


def padded(size):
    return -(-size // 8) * 8


def pack_body(spread, *refs):
    if spread:
        table_ref, refs = refs[0], refs[1:]
    own_a, own_b, prev_ref, next_ref, out = refs
    half = own_a.shape[0]
    sums = []
    for own, low in ((own_a, 0), (own_b, half)):
        total = own[...].astype(F32) + prev_ref[low : low + half].astype(F32)
        sums.append((total + next_ref[low : low + half].astype(F32)).astype(BF))
    rows = jnp.concatenate(sums, axis=0)
    if spread:
        rows = jnp.dot(table_ref[...], rows, preferred_element_type=F32).astype(BF)
    out[...] = rows


def pack_returns(own_a, own_b, from_prev, from_next, size):
    rows, dim = from_prev.shape
    wide = padded(size)
    spread = wide != size
    table = np.zeros((rows // size * wide, rows), np.float32)
    at = np.arange(rows)
    table[at // size * wide + at % size, at] = 1.0
    head = (jnp.asarray(table, BF),) if spread else ()
    return pl.pallas_call(
        functools.partial(pack_body, spread),
        out_shape=jax.ShapeDtypeStruct((rows // size * wide, dim), BF),
        compiler_params=params(38),
        name="pack_returns",
    )(*head, own_a, own_b, *in_vmem((from_prev, from_next)))


def hop_body(next_a, next_b, prev_a, prev_b, got_a, got_b, to_next, to_prev):
    half = next_a.shape[0]
    to_next[:half] = (next_a[...].astype(F32) + got_a[...].astype(F32)).astype(BF)
    to_next[half:] = next_b[...]
    to_prev[:half] = prev_a[...]
    to_prev[half:] = (prev_b[...].astype(F32) + got_b[...].astype(F32)).astype(BF)


def hop_sums(*parts):
    half, dim = parts[0].shape
    return pl.pallas_call(
        hop_body,
        out_shape=[jax.ShapeDtypeStruct((2 * half, dim), BF)] * 2,
        compiler_params=params(38),
        name="hop_sums",
    )(*parts[:4], *in_vmem(parts[4:]))


def expert_body(pieces, *refs):
    ins = refs[:pieces]
    up_a, up_b, down_a, down_b = refs[pieces : pieces + 4]
    outs = refs[pieces + 4 : 2 * pieces + 4]
    x_all, dy_all, grads = refs[2 * pieces + 4 :]
    hidden, dim = up_a.shape
    steps = hidden // HIDDEN_STEP
    low = 0
    for piece, out in zip(ins, outs):
        size = out.shape[0]
        x_all[low : low + size] = piece[:size]
        dy_all[low : low + size] = piece[size:]
        low += size
    across = (((1,), (1,)), ((), ()))

    def step(i, carry):
        at = pl.ds(pl.multiple_of(i * HIDDEN_STEP, HIDDEN_STEP), HIDDEN_STEP)
        up = jnp.concatenate([up_a[at], up_b[at]], axis=0)
        down = jnp.concatenate([down_a[at], down_b[at]], axis=0)
        pre = lax.dot_general(x_all[...], up, across, preferred_element_type=F32)
        back = lax.dot_general(dy_all[...], down, across, preferred_element_type=F32)
        sig = jax.nn.sigmoid(pre)
        grad = (back * sig * (1.0 + pre * (1.0 - sig))).astype(BF)
        grads[0, i] = grad[:, :HIDDEN_STEP]
        grads[1, i] = grad[:, HIDDEN_STEP:]
        return carry

    lax.fori_loop(0, steps, step, 0)
    grad_a, grad_b = (
        jnp.concatenate([grads[core, i] for i in range(steps)], axis=1) for core in range(2)
    )
    for left in range(0, dim, OUT_COLS):
        cols = slice(left, left + OUT_COLS)
        part = jnp.dot(grad_a, up_a[:, cols], preferred_element_type=F32)
        part += jnp.dot(grad_b, up_b[:, cols], preferred_element_type=F32)
        part = part.astype(BF)
        low = 0
        for out in outs:
            size = out.shape[0]
            out[:, cols] = part[low : low + size]
            low += size


def expert_rows(ins, weights):
    pieces = len(ins)
    dim = ins[0].shape[1]
    sizes = [piece.shape[0] // 2 for piece in ins]
    rows = sum(sizes)
    hidden = weights[0].shape[0]
    vmem = pl.BlockSpec(memory_space=pltpu.VMEM)
    return pl.pallas_call(
        functools.partial(expert_body, pieces),
        in_specs=[vmem] * (pieces + 4),
        out_specs=[vmem] * pieces,
        out_shape=[jax.ShapeDtypeStruct((size, dim), BF) for size in sizes],
        scratch_shapes=[
            pltpu.VMEM((rows, dim), BF),
            pltpu.VMEM((rows, dim), BF),
            pltpu.VMEM((2, hidden // HIDDEN_STEP, rows, HIDDEN_STEP), BF),
        ],
        compiler_params=params(30),
        cost_estimate=pl.CostEstimate(
            flops=6 * rows * 2 * hidden * dim,
            bytes_accessed=2 * (4 * hidden * dim + 3 * rows * dim),
            transcendentals=rows * 2 * hidden,
        ),
        name="expert_rows",
    )(*in_vmem(ins), *in_vmem(weights))


def weigh_pair(ids, weights, experts, capacity):
    tokens = ids.shape[0]
    at = lax.broadcasted_iota(jnp.int32, (tokens, experts), 1)
    hots = [(at == ids[:, k : k + 1]).astype(F32) for k in range(2)]
    before = (
        lax.broadcasted_iota(jnp.int32, (tokens, tokens), 1)
        < lax.broadcasted_iota(jnp.int32, (tokens, tokens), 0)
    ).astype(F32)
    earlier = jnp.dot(
        before.astype(BF), (hots[0] + hots[1]).astype(BF), preferred_element_type=F32
    )
    sizes = part_sizes(capacity)
    rows = experts * sum(padded(size) for size in sizes)
    place = lax.broadcasted_iota(jnp.int32, (tokens, rows), 1)
    table = jnp.zeros((tokens, rows), F32)
    for k in range(2):
        slot = jnp.sum(earlier * hots[k], axis=1, keepdims=True).astype(jnp.int32)
        own = ids[:, k : k + 1]
        target = jnp.where(
            slot < sizes[0],
            own * padded(sizes[0]) + slot,
            experts * padded(sizes[0]) + own * padded(sizes[1]) + slot - sizes[0],
        )
        table = table + jnp.where(place == target, weights[:, k : k + 1], 0.0)
    high = table.astype(BF)
    low = (table - high.astype(F32)).astype(BF)
    return high, low


def table_body(experts, capacity, ids_ref, weights_ref, high_ref, low_ref):
    high_ref[...], low_ref[...] = weigh_pair(
        ids_ref[...], weights_ref[...], experts, capacity
    )


def weigh_tables(ids, weights, experts, capacity):
    rows = experts * sum(padded(size) for size in part_sizes(capacity))
    return pl.pallas_call(
        functools.partial(table_body, experts, capacity),
        out_shape=[jax.ShapeDtypeStruct((ids.shape[0], rows), BF)] * 2,
        compiler_params=params(38),
        name="weigh_tables",
    )(ids, weights)


def scan_body(*refs):
    high_ref, low_ref = refs[:2]
    backs = refs[2:4]
    dout_ref, delta_ref, rate_ref, total_ref, mix_ref, drive_ref = refs[4:10]
    mid_ref, local_ref, start_ref, grad = refs[10:]
    back = jnp.concatenate([b[...] for b in backs], axis=0)
    routed = jnp.dot(high_ref[...], back, preferred_element_type=F32)
    routed += jnp.dot(low_ref[...], back, preferred_element_type=F32)
    mid = (dout_ref[...].astype(F32) + routed).astype(BF)
    mid_ref[...] = mid
    grad[...] = mid.astype(F32)
    negative = -rate_ref[...]
    tokens, cols = grad.shape
    states = negative.shape[0]
    repeat = cols // mix_ref.shape[2]

    def block(i, flow):
        low_t = pl.multiple_of((tokens // 8 - 1 - i) * 8, 8)
        grads = grad[pl.ds(low_t, 8)]
        deltas = delta_ref[pl.ds(low_t, 8)]
        rows = []
        for r in reversed(range(8)):
            drive = jnp.concatenate([drive_ref[low_t + r]] * repeat, axis=1)
            mix = jnp.concatenate([mix_ref[low_t + r]] * repeat, axis=1)
            state = drive * jnp.broadcast_to(grads[r : r + 1], (states, cols)) + flow
            rows.append(jnp.sum(mix * state, axis=0, keepdims=True))
            decay = jnp.exp(jnp.broadcast_to(deltas[r : r + 1], (states, cols)) * negative)
            flow = decay * state
        local_ref[pl.ds(low_t, 8)] = jnp.concatenate(rows[::-1], axis=0)
        return flow

    flow = lax.fori_loop(0, tokens // 8, block, jnp.zeros((states, cols), F32))
    total = jnp.broadcast_to(total_ref[...], (8, cols))
    whole_part = total.astype(BF).astype(F32)
    row = lax.broadcasted_iota(jnp.int32, (8, cols), 0)
    tail = jnp.where(row == 0, whole_part, jnp.where(row == 1, total - whole_part, 0.0))
    start_ref[...] = jnp.concatenate([flow, tail], axis=0).astype(BF)


def strip(rows, cols):
    return pl.BlockSpec((rows, cols), lambda i: (0, i))


def combine_and_scan(tables, backs, dout, delta, rate, total, mix, drive):
    tokens, dim = dout.shape
    states = rate.shape[0]
    cols = SCAN_COLS
    return pl.pallas_call(
        scan_body,
        grid=(dim // cols,),
        in_specs=[whole(*t.shape) for t in tables]
        + [strip(b.shape[0], cols) for b in backs]
        + [
            strip(tokens, cols),
            strip(tokens, cols),
            strip(states, cols),
            strip(1, cols),
            whole(*mix.shape),
            whole(*drive.shape),
        ],
        out_specs=[strip(tokens, cols), strip(tokens, cols), strip(states + 8, cols)],
        out_shape=[
            jax.ShapeDtypeStruct((tokens, dim), BF),
            jax.ShapeDtypeStruct((tokens, dim), F32),
            jax.ShapeDtypeStruct((states + 8, dim), BF),
        ],
        scratch_shapes=[pltpu.VMEM((tokens, cols), F32)],
        compiler_params=params(54),
        name="combine_and_scan",
    )(*tables, *backs, dout, delta, rate, total, mix, drive)


def reach_body(delta_ref, rate_ref, mix_ref, reach_ref, total_ref):
    delta = delta_ref[...]
    tokens, cols = delta.shape
    later = (
        lax.broadcasted_iota(jnp.int32, (tokens, tokens), 1)
        > lax.broadcasted_iota(jnp.int32, (tokens, tokens), 0)
    ).astype(F32)
    after = jnp.dot(
        later, delta, precision=lax.Precision.HIGHEST, preferred_element_type=F32
    )
    total_ref[...] = after[:1] + delta[:1]
    mix = mix_ref[...]
    for n in range(rate_ref.shape[0]):
        fade = jnp.exp(after * -jnp.broadcast_to(rate_ref[n : n + 1], (tokens, cols)))
        reach_ref[n] = (fade * jnp.broadcast_to(mix[:, n : n + 1], (tokens, cols))).astype(BF)


def reach_table(delta, rate, mix):
    tokens, dim = delta.shape
    states = rate.shape[0]
    cols = 512
    return pl.pallas_call(
        reach_body,
        grid=(dim // cols,),
        in_specs=[strip(tokens, cols), strip(states, cols), whole(*mix.shape)],
        out_specs=[
            pl.BlockSpec((states, tokens, cols), lambda i: (0, 0, i)),
            strip(1, cols),
        ],
        out_shape=[
            jax.ShapeDtypeStruct((states, tokens, dim), BF),
            jax.ShapeDtypeStruct((1, dim), F32),
        ],
        compiler_params=params(38),
        cost_estimate=pl.CostEstimate(
            flops=8 * states * tokens * dim,
            bytes_accessed=2 * states * tokens * dim,
            transcendentals=states * tokens * dim,
        ),
        name="reach_table",
    )(delta, rate, mix)


def carry_body(place_ref, starts_ref, rate_ref, local_ref, reach_ref, out_ref):
    place = place_ref[0]
    negative = -rate_ref[...]
    tokens, cols = local_ref.shape
    states = negative.shape[0]
    flow = jnp.zeros((states, cols), F32)
    for at in reversed(range(starts_ref.shape[0])):
        sent = starts_ref[at].astype(F32)
        total = sent[states : states + 1] + sent[states + 1 : states + 2]
        passed = jnp.exp(total * negative) * flow
        flow = jnp.where(at > place, sent[:states] + passed, flow)
    total = local_ref[...]
    for n in range(states):
        total += reach_ref[n].astype(F32) * flow[n : n + 1]
    out_ref[...] = total.astype(BF)


def add_carry(place, starts, rate, local, reach):
    tokens, dim = local.shape
    states = rate.shape[0]
    blocks = starts.shape[0]
    cols = SCAN_COLS
    return pl.pallas_call(
        carry_body,
        grid=(dim // cols,),
        in_specs=[
            pl.BlockSpec(memory_space=pltpu.SMEM),
            pl.BlockSpec((blocks, states + 8, cols), lambda i: (0, 0, i)),
            strip(states, cols),
            strip(tokens, cols),
            pl.BlockSpec((states, tokens, cols), lambda i: (0, 0, i)),
        ],
        out_specs=strip(tokens, cols),
        out_shape=jax.ShapeDtypeStruct((tokens, dim), BF),
        compiler_params=params(54),
        name="add_carry",
    )(place, starts, rate, local, reach)


def on_device(z_size, capacity, x_in, dout, route_ids, combine, w_up, w_down, delta, rate, bmat, cmat):
    experts = lax.axis_size("exp")
    x, dy, ids, weights = x_in[0], dout[0], route_ids[0], combine[0]
    up, down, steps = w_up[0], w_down[0], delta[0]

    def shift(value, by):
        ring = [(i, (i + by) % z_size) for i in range(z_size)]
        return lax.ppermute(value, "z", ring)

    def swap(value):
        return lax.ppermute(value, "core", [(0, 1), (1, 0)])

    def exchange(value):
        parts = value.reshape(experts, -1, value.shape[1])
        got = lax.all_to_all(parts, "exp", split_axis=0, concat_axis=0, tiled=True)
        return got.reshape(value.shape)

    sizes = part_sizes(capacity)
    sent = gather_rows(ids.T, x, dy, experts, capacity)
    up_other, down_other = swap(up), swap(down)
    got_low = exchange(sent[0])
    got_low, up_other, down_other = tie(got_low, up_other, down_other)
    both = (up, up_other, down, down_other)
    low_a, low_b = sort_messages(got_low, experts, sizes[0])
    high_a, high_b = sort_messages(exchange(sent[1]), experts, sizes[1])

    def ring(a, b):
        prev_a, next_b = shift(a, 1), shift(b, -1)
        prev_b, next_a = shift(b, 1), shift(a, -1)
        return prev_a, prev_b, next_a, next_b

    def far(prev_a, next_b):
        return shift(prev_a, 1), shift(next_b, -1)

    low = ring(low_a, low_b)
    low_far = far(low[0], low[3])
    lanes = (steps.shape[0], bmat.shape[2], 128)
    mix = jnp.broadcast_to(bmat[0][:, :, None], lanes)
    drive = jnp.broadcast_to(cmat[0][:, :, None], lanes)
    reach, total = reach_table(steps, rate, bmat[0])
    tables = weigh_tables(ids, weights, experts, capacity)
    low, reach, total, tables, mix, drive = tie(low, reach, total, tables, mix, drive)
    first = expert_rows((low_a, low_b, *low), both)
    high = ring(high_a, high_b)
    low_far, first = tie(low_far, first)
    second = expert_rows((*low_far, high_a, high_b), both)
    high, second = tie(high, second)
    high_far = far(high[0], high[3])
    third = expert_rows(high, both)
    low_sums = hop_sums(*first[4:6], *first[2:4], shift(second[0], 1), shift(second[1], -1))
    high_far, third, low_sums = tie(high_far, third, low_sums)
    fourth = expert_rows(high_far, both)

    def home(own, sums, size):
        to_next, to_prev = sums
        return pack_returns(*own, shift(to_next, 1), shift(to_prev, -1), size)

    low_home = home(first[:2], low_sums, sizes[0])
    high_got = (shift(fourth[0], 1), shift(fourth[1], -1))
    low_home, high_got = tie(low_home, high_got)
    low_back = exchange(low_home)
    high_sums = hop_sums(*third[2:4], *third[:2], *high_got)
    backs = (low_back, exchange(home(second[2:4], high_sums, sizes[1])))

    mid, local, start = combine_and_scan(
        tables, backs, dy, steps, rate, total, mix, drive
    )
    starts = lax.all_gather(start, ("z", "core"))
    place = lax.axis_index(("z", "core")).astype(jnp.int32).reshape(1)
    scan = add_carry(place, starts, rate, local, reach)
    return (mid[None], scan[None])


def solution(mesh):
    seq, exp = mesh.shape["seq"], mesh.shape["exp"]
    z_size = seq // CORES
    split = Mesh(mesh.devices.reshape(z_size, CORES, exp), ("z", "core", "exp"))
    token = P("exp", ("z", "core"), None)

    def run(x_in, dout, route_ids, *rest):
        tokens = route_ids.shape[1] // seq
        capacity = 5 * tokens * route_ids.shape[2] // (4 * exp)
        return jax.shard_map(
            functools.partial(on_device, z_size, capacity),
            mesh=split,
            in_specs=(token,) * 7 + (P(),) + (token,) * 2,
            out_specs=(token, token),
            check_vma=False,
        )(x_in, dout, route_ids, *rest)

    return run
```

```python
import functools

import jax
import jax.numpy as jnp
import numpy as np
from jax import lax
from jax.experimental import pallas as pl
from jax.experimental.pallas import tpu as pltpu
from jax.sharding import Mesh
from jax.sharding import PartitionSpec as P

CORES = 2
EARLY = 12
HIDDEN_STEP = 128
OUT_COLS = 512
SCAN_COLS = 1024
BF = jnp.bfloat16
F32 = jnp.float32


def params(mebibytes):
    return pltpu.CompilerParams(vmem_limit_bytes=mebibytes * 1024 * 1024)


def in_vmem(values):
    return [pltpu.with_memory_space_constraint(v, pltpu.VMEM) for v in values]


def whole(*shape):
    return pl.BlockSpec(shape, lambda *_: (0,) * len(shape))


def tie(*values):
    return lax.optimization_barrier(values)


def part_sizes(capacity):
    return (EARLY, capacity - EARLY)


def gather_body(capacity, ids_ref, x_ref, dy_ref, *outs):
    tokens = x_ref.shape[0]
    experts = outs[0].shape[0] // (2 * EARLY)
    ids = ids_ref[...]
    at = lax.broadcasted_iota(jnp.int32, (experts, tokens), 0)
    hots = [(at == ids[k : k + 1, :]).astype(F32) for k in range(2)]
    before = (
        lax.broadcasted_iota(jnp.int32, (tokens, tokens), 0)
        < lax.broadcasted_iota(jnp.int32, (tokens, tokens), 1)
    ).astype(F32)
    earlier = jnp.dot(
        (hots[0] + hots[1]).astype(BF), before.astype(BF), preferred_element_type=F32
    )
    slots = [
        jnp.sum(earlier * hot, axis=0, keepdims=True).astype(jnp.int32) for hot in hots
    ]
    first = 0
    for size, out in zip(part_sizes(capacity), outs):
        place = lax.broadcasted_iota(jnp.int32, (out.shape[0], tokens), 0)
        pick_x = pick_dy = None
        for k in range(2):
            slot = slots[k] - first
            inside = (slot >= 0) & (slot < size)
            target = jnp.where(inside, ids[k : k + 1, :] * (2 * size) + slot, -size - 1)
            hit_x, hit_dy = place == target, place == target + size
            pick_x = hit_x if pick_x is None else pick_x | hit_x
            pick_dy = hit_dy if pick_dy is None else pick_dy | hit_dy
        rows = jnp.dot(pick_x.astype(F32).astype(BF), x_ref[...], preferred_element_type=F32)
        rows += jnp.dot(
            pick_dy.astype(F32).astype(BF), dy_ref[...], preferred_element_type=F32
        )
        out[...] = rows.astype(BF)
        first += size


def gather_rows(ids_t, x, dy, experts, capacity):
    dim = x.shape[1]
    return pl.pallas_call(
        functools.partial(gather_body, capacity),
        out_shape=[
            jax.ShapeDtypeStruct((experts * 2 * size, dim), BF)
            for size in part_sizes(capacity)
        ],
        compiler_params=params(40),
        name="gather_rows",
    )(ids_t, x, dy)


def sort_body(table_ref, rows_ref, out):
    size = table_ref.shape[0]
    for low in range(0, out.shape[0], size):
        rows = rows_ref[low : low + size]
        out[low : low + size] = jnp.dot(
            table_ref[...], rows, preferred_element_type=F32
        ).astype(BF)


def sort_messages(messages, experts, size):
    count, dim = experts // 2, messages.shape[1]
    rows = 2 * size * count
    at = np.arange(rows)
    kind, rest = at // (size * count), at % (size * count)
    table = np.zeros((rows, rows), np.float32)
    table[at, rest // size * 2 * size + kind * size + rest % size] = 1.0
    return pl.pallas_call(
        sort_body,
        out_shape=jax.ShapeDtypeStruct((2 * rows, dim), BF),
        compiler_params=params(44),
        name="sort_messages",
    )(jnp.asarray(table, BF), *in_vmem((messages,)))


def padded(size):
    return -(-size // 8) * 8


def pack_body(spread, *refs):
    if spread:
        table_ref, refs = refs[0], refs[1:]
    own_a, own_b, prev_ref, next_ref, out = refs
    half = own_a.shape[0]
    sums = []
    for own, low in ((own_a, 0), (own_b, half)):
        total = own[...].astype(F32) + prev_ref[low : low + half].astype(F32)
        sums.append((total + next_ref[low : low + half].astype(F32)).astype(BF))
    rows = jnp.concatenate(sums, axis=0)
    if spread:
        rows = jnp.dot(table_ref[...], rows, preferred_element_type=F32).astype(BF)
    out[...] = rows


def pack_returns(own_a, own_b, from_prev, from_next, size):
    rows, dim = from_prev.shape
    wide = padded(size)
    spread = wide != size
    table = np.zeros((rows // size * wide, rows), np.float32)
    at = np.arange(rows)
    table[at // size * wide + at % size, at] = 1.0
    head = (jnp.asarray(table, BF),) if spread else ()
    return pl.pallas_call(
        functools.partial(pack_body, spread),
        out_shape=jax.ShapeDtypeStruct((rows // size * wide, dim), BF),
        compiler_params=params(38),
        name="pack_returns",
    )(*head, own_a, own_b, *in_vmem((from_prev, from_next)))


def hop_body(next_a, next_b, prev_a, prev_b, got_a, got_b, to_next, to_prev):
    half = next_a.shape[0]
    to_next[:half] = (next_a[...].astype(F32) + got_a[...].astype(F32)).astype(BF)
    to_next[half:] = next_b[...]
    to_prev[:half] = prev_a[...]
    to_prev[half:] = (prev_b[...].astype(F32) + got_b[...].astype(F32)).astype(BF)


def hop_sums(*parts):
    half, dim = parts[0].shape
    return pl.pallas_call(
        hop_body,
        out_shape=[jax.ShapeDtypeStruct((2 * half, dim), BF)] * 2,
        compiler_params=params(38),
        name="hop_sums",
    )(*parts[:4], *in_vmem(parts[4:]))


def expert_body(sizes, *refs):
    count = len(sizes)
    ins = refs[:count]
    up_a, up_b, down_a, down_b = refs[count : count + 4]
    outs = refs[count + 4 : -3]
    x_all, dy_all, grads = refs[-3:]
    hidden, dim = up_a.shape
    steps = hidden // HIDDEN_STEP
    low = 0
    for pieces, size in zip(ins, sizes):
        for top in range(0, pieces.shape[0], 2 * size):
            x_all[low : low + size] = pieces[top : top + size]
            dy_all[low : low + size] = pieces[top + size : top + 2 * size]
            low += size
    across = (((1,), (1,)), ((), ()))

    def step(i, carry):
        at = pl.ds(pl.multiple_of(i * HIDDEN_STEP, HIDDEN_STEP), HIDDEN_STEP)
        up = jnp.concatenate([up_a[at], up_b[at]], axis=0)
        down = jnp.concatenate([down_a[at], down_b[at]], axis=0)
        pre = lax.dot_general(x_all[...], up, across, preferred_element_type=F32)
        back = lax.dot_general(dy_all[...], down, across, preferred_element_type=F32)
        sig = jax.nn.sigmoid(pre)
        grad = (back * sig * (1.0 + pre * (1.0 - sig))).astype(BF)
        grads[0, i] = grad[:, :HIDDEN_STEP]
        grads[1, i] = grad[:, HIDDEN_STEP:]
        return carry

    lax.fori_loop(0, steps, step, 0)
    grad_a, grad_b = (
        jnp.concatenate([grads[core, i] for i in range(steps)], axis=1) for core in range(2)
    )
    for left in range(0, dim, OUT_COLS):
        cols = slice(left, left + OUT_COLS)
        part = jnp.dot(grad_a, up_a[:, cols], preferred_element_type=F32)
        part += jnp.dot(grad_b, up_b[:, cols], preferred_element_type=F32)
        part = part.astype(BF)
        low = 0
        for out in outs:
            size = out.shape[0]
            out[:, cols] = part[low : low + size]
            low += size


def expert_rows(ins, sizes, weights):
    dim = ins[0].shape[1]
    out_sizes = [
        size for value, size in zip(ins, sizes) for _ in range(value.shape[0] // (2 * size))
    ]
    rows = sum(out_sizes)
    hidden = weights[0].shape[0]
    vmem = pl.BlockSpec(memory_space=pltpu.VMEM)
    return pl.pallas_call(
        functools.partial(expert_body, sizes),
        in_specs=[vmem] * (len(ins) + 4),
        out_specs=[vmem] * len(out_sizes),
        out_shape=[jax.ShapeDtypeStruct((size, dim), BF) for size in out_sizes],
        scratch_shapes=[
            pltpu.VMEM((rows, dim), BF),
            pltpu.VMEM((rows, dim), BF),
            pltpu.VMEM((2, hidden // HIDDEN_STEP, rows, HIDDEN_STEP), BF),
        ],
        compiler_params=params(30),
        cost_estimate=pl.CostEstimate(
            flops=6 * rows * 2 * hidden * dim // 8,
            bytes_accessed=rows * dim,
            transcendentals=rows,
        ),
        name="expert_rows",
    )(*in_vmem(ins), *in_vmem(weights))


def weigh_pair(ids, weights, experts, capacity):
    tokens = ids.shape[0]
    at = lax.broadcasted_iota(jnp.int32, (tokens, experts), 1)
    hots = [(at == ids[:, k : k + 1]).astype(F32) for k in range(2)]
    before = (
        lax.broadcasted_iota(jnp.int32, (tokens, tokens), 1)
        < lax.broadcasted_iota(jnp.int32, (tokens, tokens), 0)
    ).astype(F32)
    earlier = jnp.dot(
        before.astype(BF), (hots[0] + hots[1]).astype(BF), preferred_element_type=F32
    )
    sizes = part_sizes(capacity)
    rows = experts * sum(padded(size) for size in sizes)
    place = lax.broadcasted_iota(jnp.int32, (tokens, rows), 1)
    table = jnp.zeros((tokens, rows), F32)
    for k in range(2):
        slot = jnp.sum(earlier * hots[k], axis=1, keepdims=True).astype(jnp.int32)
        own = ids[:, k : k + 1]
        target = jnp.where(
            slot < sizes[0],
            own * padded(sizes[0]) + slot,
            experts * padded(sizes[0]) + own * padded(sizes[1]) + slot - sizes[0],
        )
        table = table + jnp.where(place == target, weights[:, k : k + 1], 0.0)
    high = table.astype(BF)
    low = (table - high.astype(F32)).astype(BF)
    return high, low


def table_body(experts, capacity, ids_ref, weights_ref, high_ref, low_ref):
    high_ref[...], low_ref[...] = weigh_pair(
        ids_ref[...], weights_ref[...], experts, capacity
    )


def weigh_tables(ids, weights, experts, capacity):
    rows = experts * sum(padded(size) for size in part_sizes(capacity))
    return pl.pallas_call(
        functools.partial(table_body, experts, capacity),
        out_shape=[jax.ShapeDtypeStruct((ids.shape[0], rows), BF)] * 2,
        compiler_params=params(44),
        name="weigh_tables",
    )(ids, weights)


def scan_body(*refs):
    high_ref, low_ref = refs[:2]
    backs = refs[2:4]
    dout_ref, delta_ref, rate_ref, total_ref, mix_ref, drive_ref = refs[4:10]
    mid_ref, local_ref, start_ref, grad = refs[10:]
    back = jnp.concatenate([b[...] for b in backs], axis=0)
    routed = jnp.dot(high_ref[...], back, preferred_element_type=F32)
    routed += jnp.dot(low_ref[...], back, preferred_element_type=F32)
    mid = (dout_ref[...].astype(F32) + routed).astype(BF)
    mid_ref[...] = mid
    grad[...] = mid.astype(F32)
    negative = -rate_ref[...]
    tokens, cols = grad.shape
    states = negative.shape[0]
    repeat = cols // mix_ref.shape[2]

    def block(i, flow):
        low_t = pl.multiple_of((tokens // 8 - 1 - i) * 8, 8)
        grads = grad[pl.ds(low_t, 8)]
        deltas = delta_ref[pl.ds(low_t, 8)]
        rows = []
        for r in reversed(range(8)):
            drive = jnp.concatenate([drive_ref[low_t + r]] * repeat, axis=1)
            mix = jnp.concatenate([mix_ref[low_t + r]] * repeat, axis=1)
            state = drive * jnp.broadcast_to(grads[r : r + 1], (states, cols)) + flow
            rows.append(jnp.sum(mix * state, axis=0, keepdims=True))
            decay = jnp.exp(jnp.broadcast_to(deltas[r : r + 1], (states, cols)) * negative)
            flow = decay * state
        local_ref[pl.ds(low_t, 8)] = jnp.concatenate(rows[::-1], axis=0)
        return flow

    flow = lax.fori_loop(0, tokens // 8, block, jnp.zeros((states, cols), F32))
    total = jnp.broadcast_to(total_ref[...], (8, cols))
    whole_part = total.astype(BF).astype(F32)
    row = lax.broadcasted_iota(jnp.int32, (8, cols), 0)
    tail = jnp.where(row == 0, whole_part, jnp.where(row == 1, total - whole_part, 0.0))
    start_ref[...] = jnp.concatenate([flow, tail], axis=0).astype(BF)


def strip(rows, cols):
    return pl.BlockSpec((rows, cols), lambda i: (0, i))


def combine_and_scan(tables, backs, dout, delta, rate, total, mix, drive):
    tokens, dim = dout.shape
    states = rate.shape[0]
    cols = SCAN_COLS
    return pl.pallas_call(
        scan_body,
        grid=(dim // cols,),
        in_specs=[whole(*t.shape) for t in tables]
        + [strip(b.shape[0], cols) for b in backs]
        + [
            strip(tokens, cols),
            strip(tokens, cols),
            strip(states, cols),
            strip(1, cols),
            whole(*mix.shape),
            whole(*drive.shape),
        ],
        out_specs=[strip(tokens, cols), strip(tokens, cols), strip(states + 8, cols)],
        out_shape=[
            jax.ShapeDtypeStruct((tokens, dim), BF),
            jax.ShapeDtypeStruct((tokens, dim), F32),
            jax.ShapeDtypeStruct((states + 8, dim), BF),
        ],
        scratch_shapes=[pltpu.VMEM((tokens, cols), F32)],
        compiler_params=params(54),
        name="combine_and_scan",
    )(*tables, *backs, dout, delta, rate, total, mix, drive)


def reach_body(delta_ref, rate_ref, mix_ref, reach_ref, total_ref):
    delta = delta_ref[...]
    tokens, cols = delta.shape
    later = (
        lax.broadcasted_iota(jnp.int32, (tokens, tokens), 1)
        > lax.broadcasted_iota(jnp.int32, (tokens, tokens), 0)
    ).astype(F32)
    after = jnp.dot(
        later, delta, precision=lax.Precision.HIGHEST, preferred_element_type=F32
    )
    total_ref[...] = after[:1] + delta[:1]
    mix = mix_ref[...]
    for n in range(rate_ref.shape[0]):
        fade = jnp.exp(after * -jnp.broadcast_to(rate_ref[n : n + 1], (tokens, cols)))
        reach_ref[n] = (fade * jnp.broadcast_to(mix[:, n : n + 1], (tokens, cols))).astype(BF)


def reach_table(delta, rate, mix):
    tokens, dim = delta.shape
    states = rate.shape[0]
    cols = 512
    return pl.pallas_call(
        reach_body,
        grid=(dim // cols,),
        in_specs=[strip(tokens, cols), strip(states, cols), whole(*mix.shape)],
        out_specs=[
            pl.BlockSpec((states, tokens, cols), lambda i: (0, 0, i)),
            strip(1, cols),
        ],
        out_shape=[
            jax.ShapeDtypeStruct((states, tokens, dim), BF),
            jax.ShapeDtypeStruct((1, dim), F32),
        ],
        compiler_params=params(46),
        cost_estimate=pl.CostEstimate(
            flops=8 * states * tokens * dim,
            bytes_accessed=2 * states * tokens * dim,
            transcendentals=states * tokens * dim,
        ),
        name="reach_table",
    )(delta, rate, mix)


def carry_body(place_ref, starts_ref, rate_ref, local_ref, reach_ref, out_ref):
    place = place_ref[0]
    negative = -rate_ref[...]
    tokens, cols = local_ref.shape
    states = negative.shape[0]
    flow = jnp.zeros((states, cols), F32)
    for at in reversed(range(starts_ref.shape[0])):
        sent = starts_ref[at].astype(F32)
        total = sent[states : states + 1] + sent[states + 1 : states + 2]
        passed = jnp.exp(total * negative) * flow
        flow = jnp.where(at > place, sent[:states] + passed, flow)
    total = local_ref[...]
    for n in range(states):
        total += reach_ref[n].astype(F32) * flow[n : n + 1]
    out_ref[...] = total.astype(BF)


def add_carry(place, starts, rate, local, reach):
    tokens, dim = local.shape
    states = rate.shape[0]
    blocks = starts.shape[0]
    cols = SCAN_COLS
    return pl.pallas_call(
        carry_body,
        grid=(dim // cols,),
        in_specs=[
            pl.BlockSpec(memory_space=pltpu.SMEM),
            pl.BlockSpec((blocks, states + 8, cols), lambda i: (0, 0, i)),
            strip(states, cols),
            strip(tokens, cols),
            pl.BlockSpec((states, tokens, cols), lambda i: (0, 0, i)),
        ],
        out_specs=strip(tokens, cols),
        out_shape=jax.ShapeDtypeStruct((tokens, dim), BF),
        compiler_params=params(54),
        name="add_carry",
    )(place, starts, rate, local, reach)


def on_device(z_size, capacity, x_in, dout, route_ids, combine, w_up, w_down, delta, rate, bmat, cmat):
    experts = lax.axis_size("exp")
    x, dy, ids, weights = x_in[0], dout[0], route_ids[0], combine[0]
    up, down, steps = w_up[0], w_down[0], delta[0]

    def shift(value, by):
        ring = [(i, (i + by) % z_size) for i in range(z_size)]
        return lax.ppermute(value, "z", ring)

    def swap(value):
        return lax.ppermute(value, "core", [(0, 1), (1, 0)])

    def exchange(value):
        parts = value.reshape(experts, -1, value.shape[1])
        got = lax.all_to_all(parts, "exp", split_axis=0, concat_axis=0, tiled=True)
        return got.reshape(value.shape)

    sizes = part_sizes(capacity)
    sent = gather_rows(ids.T, x, dy, experts, capacity)
    up_other, down_other = swap(up), swap(down)
    got_low = exchange(sent[0])
    got_low, up_other, down_other = tie(got_low, up_other, down_other)
    both = (up, up_other, down, down_other)
    low = sort_messages(got_low, experts, sizes[0])
    got_high = exchange(sent[1])

    def ring(own):
        return shift(own, 1), shift(own, -1)

    def far(prev, next_):
        half = prev.shape[0] // 2
        return shift(prev[:half], 1), shift(next_[half:], -1)

    def some(part, count):
        return (sizes[part] * experts // 2,) * count

    low_near = ring(low)
    lanes = (steps.shape[0], bmat.shape[2], 128)
    mix = jnp.broadcast_to(bmat[0][:, :, None], lanes)
    drive = jnp.broadcast_to(cmat[0][:, :, None], lanes)
    reach, total = reach_table(steps, rate, bmat[0])
    tables = weigh_tables(ids, weights, experts, capacity)
    got_high, reach, total, tables, mix, drive = tie(
        got_high, reach, total, tables, mix, drive
    )
    high = sort_messages(got_high, experts, sizes[1])
    low_near, high = tie(low_near, high)
    low_far = far(*low_near)
    high_near = ring(high)
    first = expert_rows((low, *low_near), some(0, 3), both)
    low_far, high_near, first = tie(low_far, high_near, first)
    high_far = far(*high_near)
    second = expert_rows((*low_far, high), some(0, 2) + some(1, 1), both)
    high_near, second = tie(high_near, second)
    third = expert_rows(high_near, some(1, 2), both)
    low_sums = hop_sums(*first[4:6], *first[2:4], shift(second[0], 1), shift(second[1], -1))
    high_far, third, low_sums = tie(high_far, third, low_sums)
    fourth = expert_rows(high_far, some(1, 2), both)

    def home(own, sums, size):
        to_next, to_prev = sums
        return pack_returns(*own, shift(to_next, 1), shift(to_prev, -1), size)

    low_home = home(first[:2], low_sums, sizes[0])
    high_got = (shift(fourth[0], 1), shift(fourth[1], -1))
    low_home, high_got = tie(low_home, high_got)
    low_back = exchange(low_home)
    high_sums = hop_sums(*third[2:4], *third[:2], *high_got)
    backs = (low_back, exchange(home(second[2:4], high_sums, sizes[1])))

    mid, local, start = combine_and_scan(
        tables, backs, dy, steps, rate, total, mix, drive
    )
    starts = lax.all_gather(start, ("z", "core"))
    place = lax.axis_index(("z", "core")).astype(jnp.int32).reshape(1)
    scan = add_carry(place, starts, rate, local, reach)
    return (mid[None], scan[None])


def solution(mesh):
    seq, exp = mesh.shape["seq"], mesh.shape["exp"]
    z_size = seq // CORES
    split = Mesh(mesh.devices.reshape(z_size, CORES, exp), ("z", "core", "exp"))
    token = P("exp", ("z", "core"), None)

    def run(x_in, dout, route_ids, *rest):
        tokens = route_ids.shape[1] // seq
        capacity = 5 * tokens * route_ids.shape[2] // (4 * exp)
        return jax.shard_map(
            functools.partial(on_device, z_size, capacity),
            mesh=split,
            in_specs=(token,) * 7 + (P(),) + (token,) * 2,
            out_specs=(token, token),
            check_vma=False,
        )(x_in, dout, route_ids, *rest)

    return run
```

```python
import functools

import jax
import jax.numpy as jnp
import numpy as np
from jax import lax
from jax.experimental import pallas as pl
from jax.experimental.pallas import tpu as pltpu
from jax.sharding import Mesh
from jax.sharding import PartitionSpec as P

CORES = 2
EARLY = 12
HIDDEN_STEP = 128
OUT_COLS = 512
SCAN_COLS = 1024
BF = jnp.bfloat16
LOG2_E = 1.4426950408889634
F32 = jnp.float32


def params(mebibytes):
    return pltpu.CompilerParams(vmem_limit_bytes=mebibytes * 1024 * 1024)


def in_vmem(values):
    return [pltpu.with_memory_space_constraint(v, pltpu.VMEM) for v in values]


def whole(*shape):
    return pl.BlockSpec(shape, lambda *_: (0,) * len(shape))


def tie(*values):
    return lax.optimization_barrier(values)


def part_sizes(capacity):
    return (EARLY, capacity - EARLY)


def gather_body(capacity, ids_ref, x_ref, dy_ref, *outs):
    tokens = x_ref.shape[0]
    experts = outs[0].shape[0] // (2 * EARLY)
    ids = ids_ref[...]
    at = lax.broadcasted_iota(jnp.int32, (experts, tokens), 0)
    hots = [(at == ids[k : k + 1, :]).astype(F32) for k in range(2)]
    before = (
        lax.broadcasted_iota(jnp.int32, (tokens, tokens), 0)
        < lax.broadcasted_iota(jnp.int32, (tokens, tokens), 1)
    ).astype(F32)
    earlier = jnp.dot(
        (hots[0] + hots[1]).astype(BF), before.astype(BF), preferred_element_type=F32
    )
    slots = [
        jnp.sum(earlier * hot, axis=0, keepdims=True).astype(jnp.int32) for hot in hots
    ]
    first = 0
    for size, out in zip(part_sizes(capacity), outs):
        place = lax.broadcasted_iota(jnp.int32, (out.shape[0], tokens), 0)
        pick_x = pick_dy = None
        for k in range(2):
            slot = slots[k] - first
            inside = (slot >= 0) & (slot < size)
            target = jnp.where(inside, ids[k : k + 1, :] * (2 * size) + slot, -size - 1)
            hit_x, hit_dy = place == target, place == target + size
            pick_x = hit_x if pick_x is None else pick_x | hit_x
            pick_dy = hit_dy if pick_dy is None else pick_dy | hit_dy
        rows = jnp.dot(pick_x.astype(F32).astype(BF), x_ref[...], preferred_element_type=F32)
        rows += jnp.dot(
            pick_dy.astype(F32).astype(BF), dy_ref[...], preferred_element_type=F32
        )
        out[...] = rows.astype(BF)
        first += size


def gather_rows(ids_t, x, dy, experts, capacity):
    dim = x.shape[1]
    return pl.pallas_call(
        functools.partial(gather_body, capacity),
        out_shape=[
            jax.ShapeDtypeStruct((experts * 2 * size, dim), BF)
            for size in part_sizes(capacity)
        ],
        compiler_params=params(40),
        name="gather_rows",
    )(ids_t, x, dy)


def sort_body(table_ref, rows_ref, out):
    size = table_ref.shape[0]
    for low in range(0, out.shape[0], size):
        rows = rows_ref[low : low + size]
        out[low : low + size] = jnp.dot(
            table_ref[...], rows, preferred_element_type=F32
        ).astype(BF)


def sort_messages(messages, experts, size):
    count, dim = experts // 2, messages.shape[1]
    rows = 2 * size * count
    at = np.arange(rows)
    kind, rest = at // (size * count), at % (size * count)
    table = np.zeros((rows, rows), np.float32)
    table[at, rest // size * 2 * size + kind * size + rest % size] = 1.0
    return pl.pallas_call(
        sort_body,
        out_shape=jax.ShapeDtypeStruct((2 * rows, dim), BF),
        compiler_params=params(44),
        name="sort_messages",
    )(jnp.asarray(table, BF), *in_vmem((messages,)))


def padded(size):
    return -(-size // 8) * 8


def pack_body(spread, *refs):
    if spread:
        table_ref, refs = refs[0], refs[1:]
    own_a, own_b, prev_ref, next_ref, out = refs
    half = own_a.shape[0]
    sums = []
    for own, low in ((own_a, 0), (own_b, half)):
        total = own[...].astype(F32) + prev_ref[low : low + half].astype(F32)
        sums.append((total + next_ref[low : low + half].astype(F32)).astype(BF))
    rows = jnp.concatenate(sums, axis=0)
    if spread:
        rows = jnp.dot(table_ref[...], rows, preferred_element_type=F32).astype(BF)
    out[...] = rows


def pack_returns(own_a, own_b, from_prev, from_next, size):
    rows, dim = from_prev.shape
    wide = padded(size)
    spread = wide != size
    table = np.zeros((rows // size * wide, rows), np.float32)
    at = np.arange(rows)
    table[at // size * wide + at % size, at] = 1.0
    head = (jnp.asarray(table, BF),) if spread else ()
    return pl.pallas_call(
        functools.partial(pack_body, spread),
        out_shape=jax.ShapeDtypeStruct((rows // size * wide, dim), BF),
        compiler_params=params(38),
        name="pack_returns",
    )(*head, own_a, own_b, *in_vmem((from_prev, from_next)))


def hop_body(next_a, next_b, prev_a, prev_b, got_a, got_b, to_next, to_prev):
    half = next_a.shape[0]
    to_next[:half] = (next_a[...].astype(F32) + got_a[...].astype(F32)).astype(BF)
    to_next[half:] = next_b[...]
    to_prev[:half] = prev_a[...]
    to_prev[half:] = (prev_b[...].astype(F32) + got_b[...].astype(F32)).astype(BF)


def hop_sums(*parts):
    half, dim = parts[0].shape
    return pl.pallas_call(
        hop_body,
        out_shape=[jax.ShapeDtypeStruct((2 * half, dim), BF)] * 2,
        compiler_params=params(38),
        name="hop_sums",
    )(*parts[:4], *in_vmem(parts[4:]))


def expert_body(sizes, *refs):
    count = len(sizes)
    ins = refs[:count]
    up_a, up_b, down_a, down_b = refs[count : count + 4]
    outs = refs[count + 4 : -3]
    x_all, dy_all, grads = refs[-3:]
    hidden, dim = up_a.shape
    steps = hidden // HIDDEN_STEP
    low = 0
    for pieces, size in zip(ins, sizes):
        for top in range(0, pieces.shape[0], 2 * size):
            x_all[low : low + size] = pieces[top : top + size]
            dy_all[low : low + size] = pieces[top + size : top + 2 * size]
            low += size
    across = (((1,), (1,)), ((), ()))

    def step(i, carry):
        at = pl.ds(pl.multiple_of(i * HIDDEN_STEP, HIDDEN_STEP), HIDDEN_STEP)
        up = jnp.concatenate([up_a[at], up_b[at]], axis=0)
        down = jnp.concatenate([down_a[at], down_b[at]], axis=0)
        pre = lax.dot_general(x_all[...], up, across, preferred_element_type=F32)
        back = lax.dot_general(dy_all[...], down, across, preferred_element_type=F32)
        sig = jax.nn.sigmoid(pre)
        grad = (back * sig * (1.0 + pre * (1.0 - sig))).astype(BF)
        grads[0, i] = grad[:, :HIDDEN_STEP]
        grads[1, i] = grad[:, HIDDEN_STEP:]
        return carry

    lax.fori_loop(0, steps, step, 0)
    grad_a, grad_b = (
        jnp.concatenate([grads[core, i] for i in range(steps)], axis=1) for core in range(2)
    )
    for left in range(0, dim, OUT_COLS):
        cols = slice(left, left + OUT_COLS)
        part = jnp.dot(grad_a, up_a[:, cols], preferred_element_type=F32)
        part += jnp.dot(grad_b, up_b[:, cols], preferred_element_type=F32)
        part = part.astype(BF)
        low = 0
        for out in outs:
            size = out.shape[0]
            out[:, cols] = part[low : low + size]
            low += size


def expert_rows(ins, sizes, weights):
    dim = ins[0].shape[1]
    out_sizes = [
        size for value, size in zip(ins, sizes) for _ in range(value.shape[0] // (2 * size))
    ]
    rows = sum(out_sizes)
    hidden = weights[0].shape[0]
    vmem = pl.BlockSpec(memory_space=pltpu.VMEM)
    return pl.pallas_call(
        functools.partial(expert_body, sizes),
        in_specs=[vmem] * (len(ins) + 4),
        out_specs=[vmem] * len(out_sizes),
        out_shape=[jax.ShapeDtypeStruct((size, dim), BF) for size in out_sizes],
        scratch_shapes=[
            pltpu.VMEM((rows, dim), BF),
            pltpu.VMEM((rows, dim), BF),
            pltpu.VMEM((2, hidden // HIDDEN_STEP, rows, HIDDEN_STEP), BF),
        ],
        compiler_params=params(30),
        cost_estimate=pl.CostEstimate(
            flops=6 * rows * 2 * hidden * dim // 8,
            bytes_accessed=rows * dim,
            transcendentals=rows,
        ),
        name="expert_rows",
    )(*in_vmem(ins), *in_vmem(weights))


def weigh_pair(ids, weights, experts, capacity):
    tokens = ids.shape[0]
    at = lax.broadcasted_iota(jnp.int32, (tokens, experts), 1)
    hots = [(at == ids[:, k : k + 1]).astype(F32) for k in range(2)]
    before = (
        lax.broadcasted_iota(jnp.int32, (tokens, tokens), 1)
        < lax.broadcasted_iota(jnp.int32, (tokens, tokens), 0)
    ).astype(F32)
    earlier = jnp.dot(
        before.astype(BF), (hots[0] + hots[1]).astype(BF), preferred_element_type=F32
    )
    sizes = part_sizes(capacity)
    rows = experts * sum(padded(size) for size in sizes)
    place = lax.broadcasted_iota(jnp.int32, (tokens, rows), 1)
    table = jnp.zeros((tokens, rows), F32)
    for k in range(2):
        slot = jnp.sum(earlier * hots[k], axis=1, keepdims=True).astype(jnp.int32)
        own = ids[:, k : k + 1]
        target = jnp.where(
            slot < sizes[0],
            own * padded(sizes[0]) + slot,
            experts * padded(sizes[0]) + own * padded(sizes[1]) + slot - sizes[0],
        )
        table = table + jnp.where(place == target, weights[:, k : k + 1], 0.0)
    high = table.astype(BF)
    low = (table - high.astype(F32)).astype(BF)
    return high, low


def table_body(experts, capacity, ids_ref, weights_ref, high_ref, low_ref):
    high_ref[...], low_ref[...] = weigh_pair(
        ids_ref[...], weights_ref[...], experts, capacity
    )


def weigh_tables(ids, weights, experts, capacity):
    rows = experts * sum(padded(size) for size in part_sizes(capacity))
    return pl.pallas_call(
        functools.partial(table_body, experts, capacity),
        out_shape=[jax.ShapeDtypeStruct((ids.shape[0], rows), BF)] * 2,
        compiler_params=params(44),
        name="weigh_tables",
    )(ids, weights)


def scan_body(*refs):
    high_ref, low_ref = refs[:2]
    backs = refs[2:4]
    dout_ref, delta_ref, rate_ref, total_ref, mix_ref, drive_ref = refs[4:10]
    mid_ref, local_ref, start_ref, grad = refs[10:]
    back = jnp.concatenate([b[...] for b in backs], axis=0)
    routed = jnp.dot(high_ref[...], back, preferred_element_type=F32)
    routed += jnp.dot(low_ref[...], back, preferred_element_type=F32)
    mid = (dout_ref[...].astype(F32) + routed).astype(BF)
    mid_ref[...] = mid
    grad[...] = mid.astype(F32)
    negative = rate_ref[...] * -LOG2_E
    tokens, cols = grad.shape
    states = negative.shape[0]
    repeat = cols // mix_ref.shape[2]

    def block(i, flow):
        low_t = pl.multiple_of((tokens // 8 - 1 - i) * 8, 8)
        grads = grad[pl.ds(low_t, 8)]
        deltas = delta_ref[pl.ds(low_t, 8)]
        rows = []
        for r in reversed(range(8)):
            drive = jnp.concatenate([drive_ref[low_t + r]] * repeat, axis=1)
            mix = jnp.concatenate([mix_ref[low_t + r]] * repeat, axis=1)
            state = drive * jnp.broadcast_to(grads[r : r + 1], (states, cols)) + flow
            rows.append(jnp.sum(mix * state, axis=0, keepdims=True))
            decay = jnp.exp2(jnp.broadcast_to(deltas[r : r + 1], (states, cols)) * negative)
            flow = decay * state
        local_ref[pl.ds(low_t, 8)] = jnp.concatenate(rows[::-1], axis=0)
        return flow

    flow = lax.fori_loop(0, tokens // 8, block, jnp.zeros((states, cols), F32))
    total = jnp.broadcast_to(total_ref[...], (8, cols))
    whole_part = total.astype(BF).astype(F32)
    row = lax.broadcasted_iota(jnp.int32, (8, cols), 0)
    tail = jnp.where(row == 0, whole_part, jnp.where(row == 1, total - whole_part, 0.0))
    start_ref[...] = jnp.concatenate([flow, tail], axis=0).astype(BF)


def strip(rows, cols):
    return pl.BlockSpec((rows, cols), lambda i: (0, i))


def combine_and_scan(tables, backs, dout, delta, rate, total, mix, drive):
    tokens, dim = dout.shape
    states = rate.shape[0]
    cols = SCAN_COLS
    return pl.pallas_call(
        scan_body,
        grid=(dim // cols,),
        in_specs=[whole(*t.shape) for t in tables]
        + [strip(b.shape[0], cols) for b in backs]
        + [
            strip(tokens, cols),
            strip(tokens, cols),
            strip(states, cols),
            strip(1, cols),
            whole(*mix.shape),
            whole(*drive.shape),
        ],
        out_specs=[strip(tokens, cols), strip(tokens, cols), strip(states + 8, cols)],
        out_shape=[
            jax.ShapeDtypeStruct((tokens, dim), BF),
            jax.ShapeDtypeStruct((tokens, dim), F32),
            jax.ShapeDtypeStruct((states + 8, dim), BF),
        ],
        scratch_shapes=[pltpu.VMEM((tokens, cols), F32)],
        compiler_params=params(54),
        name="combine_and_scan",
    )(*tables, *backs, dout, delta, rate, total, mix, drive)


def reach_body(delta_ref, rate_ref, mix_ref, reach_ref, total_ref):
    delta = delta_ref[...]
    tokens, cols = delta.shape
    later = (
        lax.broadcasted_iota(jnp.int32, (tokens, tokens), 1)
        > lax.broadcasted_iota(jnp.int32, (tokens, tokens), 0)
    ).astype(F32)
    after = jnp.dot(
        later, delta, precision=lax.Precision.HIGHEST, preferred_element_type=F32
    )
    total_ref[...] = after[:1] + delta[:1]
    mix = mix_ref[...]
    for n in range(rate_ref.shape[0]):
        fade = jnp.exp(after * -jnp.broadcast_to(rate_ref[n : n + 1], (tokens, cols)))
        reach_ref[n] = (fade * jnp.broadcast_to(mix[:, n : n + 1], (tokens, cols))).astype(BF)


def reach_table(delta, rate, mix):
    tokens, dim = delta.shape
    states = rate.shape[0]
    cols = 512
    return pl.pallas_call(
        reach_body,
        grid=(dim // cols,),
        in_specs=[strip(tokens, cols), strip(states, cols), whole(*mix.shape)],
        out_specs=[
            pl.BlockSpec((states, tokens, cols), lambda i: (0, 0, i)),
            strip(1, cols),
        ],
        out_shape=[
            jax.ShapeDtypeStruct((states, tokens, dim), BF),
            jax.ShapeDtypeStruct((1, dim), F32),
        ],
        compiler_params=params(46),
        cost_estimate=pl.CostEstimate(
            flops=8 * states * tokens * dim,
            bytes_accessed=2 * states * tokens * dim,
            transcendentals=states * tokens * dim,
        ),
        name="reach_table",
    )(delta, rate, mix)


def carry_body(place_ref, starts_ref, rate_ref, local_ref, reach_ref, out_ref):
    place = place_ref[0]
    negative = -rate_ref[...]
    tokens, cols = local_ref.shape
    states = negative.shape[0]
    flow = jnp.zeros((states, cols), F32)
    for at in reversed(range(starts_ref.shape[0])):
        sent = starts_ref[at].astype(F32)
        total = sent[states : states + 1] + sent[states + 1 : states + 2]
        passed = jnp.exp(total * negative) * flow
        flow = jnp.where(at > place, sent[:states] + passed, flow)
    total = local_ref[...]
    for n in range(states):
        total += reach_ref[n].astype(F32) * flow[n : n + 1]
    out_ref[...] = total.astype(BF)


def add_carry(place, starts, rate, local, reach):
    tokens, dim = local.shape
    states = rate.shape[0]
    blocks = starts.shape[0]
    cols = SCAN_COLS
    return pl.pallas_call(
        carry_body,
        grid=(dim // cols,),
        in_specs=[
            pl.BlockSpec(memory_space=pltpu.SMEM),
            pl.BlockSpec((blocks, states + 8, cols), lambda i: (0, 0, i)),
            strip(states, cols),
            strip(tokens, cols),
            pl.BlockSpec((states, tokens, cols), lambda i: (0, 0, i)),
        ],
        out_specs=strip(tokens, cols),
        out_shape=jax.ShapeDtypeStruct((tokens, dim), BF),
        compiler_params=params(54),
        name="add_carry",
    )(place, starts, rate, local, reach)


def on_device(z_size, capacity, x_in, dout, route_ids, combine, w_up, w_down, delta, rate, bmat, cmat):
    experts = lax.axis_size("exp")
    x, dy, ids, weights = x_in[0], dout[0], route_ids[0], combine[0]
    up, down, steps = w_up[0], w_down[0], delta[0]

    def shift(value, by):
        ring = [(i, (i + by) % z_size) for i in range(z_size)]
        return lax.ppermute(value, "z", ring)

    def swap(value):
        return lax.ppermute(value, "core", [(0, 1), (1, 0)])

    def exchange(value):
        parts = value.reshape(experts, -1, value.shape[1])
        got = lax.all_to_all(parts, "exp", split_axis=0, concat_axis=0, tiled=True)
        return got.reshape(value.shape)

    sizes = part_sizes(capacity)
    sent = gather_rows(ids.T, x, dy, experts, capacity)
    up_other, down_other = swap(up), swap(down)
    got_low = exchange(sent[0])
    got_low, up_other, down_other = tie(got_low, up_other, down_other)
    both = (up, up_other, down, down_other)
    low = sort_messages(got_low, experts, sizes[0])
    got_high = exchange(sent[1])

    def ring(own):
        return shift(own, 1), shift(own, -1)

    def halves(prev, next_):
        half = prev.shape[0] // 2
        return prev[:half], next_[half:]

    def far(low_half, high_half):
        return shift(low_half, 1), shift(high_half, -1)

    def some(part, count):
        return (sizes[part] * experts // 2,) * count

    low_near = ring(low)
    lanes = (steps.shape[0], bmat.shape[2], 128)
    mix = jnp.broadcast_to(bmat[0][:, :, None], lanes)
    drive = jnp.broadcast_to(cmat[0][:, :, None], lanes)
    reach, total = reach_table(steps, rate, bmat[0])
    tables = weigh_tables(ids, weights, experts, capacity)
    got_high, reach, total, tables, mix, drive = tie(
        got_high, reach, total, tables, mix, drive
    )
    high = sort_messages(got_high, experts, sizes[1])
    low_near, low_halves, high = tie(low_near, halves(*low_near), high)
    low_far = far(*low_halves)
    high_near = ring(high)
    first = expert_rows((low, *low_near), some(0, 3), both)
    low_far, first = tie(low_far, first)
    second = expert_rows((*low_far, high), some(0, 2) + some(1, 1), both)
    high_near, second = tie(high_near, second)
    high_far = far(*halves(*high_near))
    third = expert_rows(high_near, some(1, 2), both)
    low_sums = hop_sums(*first[4:6], *first[2:4], shift(second[0], 1), shift(second[1], -1))
    high_far, third, low_sums = tie(high_far, third, low_sums)
    fourth = expert_rows(high_far, some(1, 2), both)

    def home(own, sums, size):
        to_next, to_prev = sums
        return pack_returns(*own, shift(to_next, 1), shift(to_prev, -1), size)

    low_home = home(first[:2], low_sums, sizes[0])
    high_got = (shift(fourth[0], 1), shift(fourth[1], -1))
    low_home, high_got = tie(low_home, high_got)
    low_back = exchange(low_home)
    high_sums = hop_sums(*third[2:4], *third[:2], *high_got)
    backs = (low_back, exchange(home(second[2:4], high_sums, sizes[1])))

    mid, local, start = combine_and_scan(
        tables, backs, dy, steps, rate, total, mix, drive
    )
    starts = lax.all_gather(start, ("z", "core"))
    place = lax.axis_index(("z", "core")).astype(jnp.int32).reshape(1)
    scan = add_carry(place, starts, rate, local, reach)
    return (mid[None], scan[None])


def solution(mesh):
    seq, exp = mesh.shape["seq"], mesh.shape["exp"]
    z_size = seq // CORES
    split = Mesh(mesh.devices.reshape(z_size, CORES, exp), ("z", "core", "exp"))
    token = P("exp", ("z", "core"), None)

    def run(x_in, dout, route_ids, *rest):
        tokens = route_ids.shape[1] // seq
        capacity = 5 * tokens * route_ids.shape[2] // (4 * exp)
        return jax.shard_map(
            functools.partial(on_device, z_size, capacity),
            mesh=split,
            in_specs=(token,) * 7 + (P(),) + (token,) * 2,
            out_specs=(token, token),
            check_vma=False,
        )(x_in, dout, route_ids, *rest)

    return run
```

```python
import functools

import jax
import jax.numpy as jnp
import numpy as np
from jax import lax
from jax.experimental import pallas as pl
from jax.experimental.pallas import tpu as pltpu
from jax.sharding import Mesh
from jax.sharding import PartitionSpec as P

CORES = 2
EARLY = 12
HIDDEN_STEP = 128
OUT_COLS = 512
SCAN_COLS = 1024
BF = jnp.bfloat16
F32 = jnp.float32


def params(mebibytes):
    return pltpu.CompilerParams(vmem_limit_bytes=mebibytes * 1024 * 1024)


def in_vmem(values):
    return [pltpu.with_memory_space_constraint(v, pltpu.VMEM) for v in values]


def whole(*shape):
    return pl.BlockSpec(shape, lambda *_: (0,) * len(shape))


def tie(*values):
    return lax.optimization_barrier(values)


def part_sizes(capacity):
    return (EARLY, capacity - EARLY)


def gather_body(capacity, ids_ref, x_ref, dy_ref, *outs):
    tokens = x_ref.shape[0]
    experts = outs[0].shape[0] // (2 * EARLY)
    ids = ids_ref[...]
    at = lax.broadcasted_iota(jnp.int32, (experts, tokens), 0)
    hots = [(at == ids[k : k + 1, :]).astype(F32) for k in range(2)]
    before = (
        lax.broadcasted_iota(jnp.int32, (tokens, tokens), 0)
        < lax.broadcasted_iota(jnp.int32, (tokens, tokens), 1)
    ).astype(F32)
    earlier = jnp.dot(
        (hots[0] + hots[1]).astype(BF), before.astype(BF), preferred_element_type=F32
    )
    slots = [
        jnp.sum(earlier * hot, axis=0, keepdims=True).astype(jnp.int32) for hot in hots
    ]
    first = 0
    for size, out in zip(part_sizes(capacity), outs):
        place = lax.broadcasted_iota(jnp.int32, (out.shape[0], tokens), 0)
        pick_x = pick_dy = None
        for k in range(2):
            slot = slots[k] - first
            inside = (slot >= 0) & (slot < size)
            target = jnp.where(inside, ids[k : k + 1, :] * (2 * size) + slot, -size - 1)
            hit_x, hit_dy = place == target, place == target + size
            pick_x = hit_x if pick_x is None else pick_x | hit_x
            pick_dy = hit_dy if pick_dy is None else pick_dy | hit_dy
        rows = jnp.dot(pick_x.astype(F32).astype(BF), x_ref[...], preferred_element_type=F32)
        rows += jnp.dot(
            pick_dy.astype(F32).astype(BF), dy_ref[...], preferred_element_type=F32
        )
        out[...] = rows.astype(BF)
        first += size


def gather_rows(ids_t, x, dy, experts, capacity):
    dim = x.shape[1]
    return pl.pallas_call(
        functools.partial(gather_body, capacity),
        out_shape=[
            jax.ShapeDtypeStruct((experts * 2 * size, dim), BF)
            for size in part_sizes(capacity)
        ],
        compiler_params=params(40),
        name="gather_rows",
    )(ids_t, x, dy)


def sort_body(table_ref, rows_ref, out):
    size = table_ref.shape[0]
    for low in range(0, out.shape[0], size):
        rows = rows_ref[low : low + size]
        out[low : low + size] = jnp.dot(
            table_ref[...], rows, preferred_element_type=F32
        ).astype(BF)


def sort_messages(messages, experts, size):
    count, dim = experts // 2, messages.shape[1]
    rows = 2 * size * count
    at = np.arange(rows)
    kind, rest = at // (size * count), at % (size * count)
    table = np.zeros((rows, rows), np.float32)
    table[at, rest // size * 2 * size + kind * size + rest % size] = 1.0
    return pl.pallas_call(
        sort_body,
        out_shape=jax.ShapeDtypeStruct((2 * rows, dim), BF),
        compiler_params=params(44),
        name="sort_messages",
    )(jnp.asarray(table, BF), *in_vmem((messages,)))


def padded(size):
    return -(-size // 8) * 8


def pack_body(spread, *refs):
    if spread:
        table_ref, refs = refs[0], refs[1:]
    own_a, own_b, prev_ref, next_ref, out = refs
    half = own_a.shape[0]
    sums = []
    for own, low in ((own_a, 0), (own_b, half)):
        total = own[...].astype(F32) + prev_ref[low : low + half].astype(F32)
        sums.append((total + next_ref[low : low + half].astype(F32)).astype(BF))
    rows = jnp.concatenate(sums, axis=0)
    if spread:
        rows = jnp.dot(table_ref[...], rows, preferred_element_type=F32).astype(BF)
    out[...] = rows


def pack_returns(own_a, own_b, from_prev, from_next, size):
    rows, dim = from_prev.shape
    wide = padded(size)
    spread = wide != size
    table = np.zeros((rows // size * wide, rows), np.float32)
    at = np.arange(rows)
    table[at // size * wide + at % size, at] = 1.0
    head = (jnp.asarray(table, BF),) if spread else ()
    return pl.pallas_call(
        functools.partial(pack_body, spread),
        out_shape=jax.ShapeDtypeStruct((rows // size * wide, dim), BF),
        compiler_params=params(16),
        name="pack_returns",
    )(*head, own_a, own_b, *in_vmem((from_prev, from_next)))


def hop_body(next_a, next_b, prev_a, prev_b, got_a, got_b, to_next, to_prev):
    half = next_a.shape[0]
    to_next[:half] = (next_a[...].astype(F32) + got_a[...].astype(F32)).astype(BF)
    to_next[half:] = next_b[...]
    to_prev[:half] = prev_a[...]
    to_prev[half:] = (prev_b[...].astype(F32) + got_b[...].astype(F32)).astype(BF)


def hop_sums(*parts):
    half, dim = parts[0].shape
    return pl.pallas_call(
        hop_body,
        out_shape=[jax.ShapeDtypeStruct((2 * half, dim), BF)] * 2,
        compiler_params=params(16),
        name="hop_sums",
    )(*parts[:4], *in_vmem(parts[4:]))


def expert_body(sizes, *refs):
    count = len(sizes)
    ins = refs[:count]
    up_a, up_b, down_a, down_b = refs[count : count + 4]
    outs = refs[count + 4 : -3]
    x_all, dy_all, grads = refs[-3:]
    hidden, dim = up_a.shape
    steps = hidden // HIDDEN_STEP
    low = 0
    for pieces, size in zip(ins, sizes):
        for top in range(0, pieces.shape[0], 2 * size):
            x_all[low : low + size] = pieces[top : top + size]
            dy_all[low : low + size] = pieces[top + size : top + 2 * size]
            low += size
    across = (((1,), (1,)), ((), ()))

    def step(i, carry):
        at = pl.ds(pl.multiple_of(i * HIDDEN_STEP, HIDDEN_STEP), HIDDEN_STEP)
        up = jnp.concatenate([up_a[at], up_b[at]], axis=0)
        down = jnp.concatenate([down_a[at], down_b[at]], axis=0)
        pre = lax.dot_general(x_all[...], up, across, preferred_element_type=F32)
        back = lax.dot_general(dy_all[...], down, across, preferred_element_type=F32)
        sig = jax.nn.sigmoid(pre)
        grad = (back * sig * (1.0 + pre * (1.0 - sig))).astype(BF)
        grads[0, i] = grad[:, :HIDDEN_STEP]
        grads[1, i] = grad[:, HIDDEN_STEP:]
        return carry

    lax.fori_loop(0, steps, step, 0)
    grad_a, grad_b = (
        jnp.concatenate([grads[core, i] for i in range(steps)], axis=1) for core in range(2)
    )
    for left in range(0, dim, OUT_COLS):
        cols = slice(left, left + OUT_COLS)
        part = jnp.dot(grad_a, up_a[:, cols], preferred_element_type=F32)
        part += jnp.dot(grad_b, up_b[:, cols], preferred_element_type=F32)
        part = part.astype(BF)
        low = 0
        for out in outs:
            size = out.shape[0]
            out[:, cols] = part[low : low + size]
            low += size


def expert_rows(ins, sizes, weights):
    dim = ins[0].shape[1]
    out_sizes = [
        size for value, size in zip(ins, sizes) for _ in range(value.shape[0] // (2 * size))
    ]
    rows = sum(out_sizes)
    hidden = weights[0].shape[0]
    vmem = pl.BlockSpec(memory_space=pltpu.VMEM)
    return pl.pallas_call(
        functools.partial(expert_body, sizes),
        in_specs=[vmem] * (len(ins) + 4),
        out_specs=[vmem] * len(out_sizes),
        out_shape=[jax.ShapeDtypeStruct((size, dim), BF) for size in out_sizes],
        scratch_shapes=[
            pltpu.VMEM((rows, dim), BF),
            pltpu.VMEM((rows, dim), BF),
            pltpu.VMEM((2, hidden // HIDDEN_STEP, rows, HIDDEN_STEP), BF),
        ],
        compiler_params=params(24),
        cost_estimate=pl.CostEstimate(
            flops=6 * rows * 2 * hidden * dim // 8,
            bytes_accessed=rows * dim,
            transcendentals=rows,
        ),
        name="expert_rows",
    )(*in_vmem(ins), *in_vmem(weights))


def weigh_pair(ids, weights, experts, capacity):
    tokens = ids.shape[0]
    at = lax.broadcasted_iota(jnp.int32, (tokens, experts), 1)
    hots = [(at == ids[:, k : k + 1]).astype(F32) for k in range(2)]
    before = (
        lax.broadcasted_iota(jnp.int32, (tokens, tokens), 1)
        < lax.broadcasted_iota(jnp.int32, (tokens, tokens), 0)
    ).astype(F32)
    earlier = jnp.dot(
        before.astype(BF), (hots[0] + hots[1]).astype(BF), preferred_element_type=F32
    )
    sizes = part_sizes(capacity)
    rows = experts * sum(padded(size) for size in sizes)
    place = lax.broadcasted_iota(jnp.int32, (tokens, rows), 1)
    table = jnp.zeros((tokens, rows), F32)
    for k in range(2):
        slot = jnp.sum(earlier * hots[k], axis=1, keepdims=True).astype(jnp.int32)
        own = ids[:, k : k + 1]
        target = jnp.where(
            slot < sizes[0],
            own * padded(sizes[0]) + slot,
            experts * padded(sizes[0]) + own * padded(sizes[1]) + slot - sizes[0],
        )
        table = table + jnp.where(place == target, weights[:, k : k + 1], 0.0)
    high = table.astype(BF)
    low = (table - high.astype(F32)).astype(BF)
    return high, low


def table_body(experts, capacity, ids_ref, weights_ref, high_ref, low_ref):
    high_ref[...], low_ref[...] = weigh_pair(
        ids_ref[...], weights_ref[...], experts, capacity
    )


def weigh_tables(ids, weights, experts, capacity):
    rows = experts * sum(padded(size) for size in part_sizes(capacity))
    return pl.pallas_call(
        functools.partial(table_body, experts, capacity),
        out_shape=[jax.ShapeDtypeStruct((ids.shape[0], rows), BF)] * 2,
        compiler_params=params(44),
        name="weigh_tables",
    )(ids, weights)


def scan_body(*refs):
    high_ref, low_ref = refs[:2]
    backs = refs[2:4]
    dout_ref, delta_ref, rate_ref, total_ref, mix_ref, drive_ref = refs[4:10]
    mid_ref, local_ref, start_ref, grad = refs[10:]
    back = jnp.concatenate([b[...] for b in backs], axis=0)
    routed = jnp.dot(high_ref[...], back, preferred_element_type=F32)
    routed += jnp.dot(low_ref[...], back, preferred_element_type=F32)
    mid = (dout_ref[...].astype(F32) + routed).astype(BF)
    mid_ref[...] = mid
    grad[...] = mid.astype(F32)
    negative = -rate_ref[...]
    tokens, cols = grad.shape
    states = negative.shape[0]
    repeat = cols // mix_ref.shape[2]

    def block(i, flow):
        low_t = pl.multiple_of((tokens // 8 - 1 - i) * 8, 8)
        grads = grad[pl.ds(low_t, 8)]
        deltas = delta_ref[pl.ds(low_t, 8)]
        rows = []
        for r in reversed(range(8)):
            drive = jnp.concatenate([drive_ref[low_t + r]] * repeat, axis=1)
            mix = jnp.concatenate([mix_ref[low_t + r]] * repeat, axis=1)
            state = drive * jnp.broadcast_to(grads[r : r + 1], (states, cols)) + flow
            rows.append(jnp.sum(mix * state, axis=0, keepdims=True))
            decay = jnp.exp(jnp.broadcast_to(deltas[r : r + 1], (states, cols)) * negative)
            flow = decay * state
        local_ref[pl.ds(low_t, 8)] = jnp.concatenate(rows[::-1], axis=0)
        return flow

    flow = lax.fori_loop(0, tokens // 8, block, jnp.zeros((states, cols), F32))
    total = jnp.broadcast_to(total_ref[...], (8, cols))
    whole_part = total.astype(BF).astype(F32)
    row = lax.broadcasted_iota(jnp.int32, (8, cols), 0)
    tail = jnp.where(row == 0, whole_part, jnp.where(row == 1, total - whole_part, 0.0))
    start_ref[...] = jnp.concatenate([flow, tail], axis=0).astype(BF)


def strip(rows, cols):
    return pl.BlockSpec((rows, cols), lambda i: (0, i))


def combine_and_scan(tables, backs, dout, delta, rate, total, mix, drive):
    tokens, dim = dout.shape
    states = rate.shape[0]
    cols = SCAN_COLS
    return pl.pallas_call(
        scan_body,
        grid=(dim // cols,),
        in_specs=[whole(*t.shape) for t in tables]
        + [strip(b.shape[0], cols) for b in backs]
        + [
            strip(tokens, cols),
            strip(tokens, cols),
            strip(states, cols),
            strip(1, cols),
            whole(*mix.shape),
            whole(*drive.shape),
        ],
        out_specs=[strip(tokens, cols), strip(tokens, cols), strip(states + 8, cols)],
        out_shape=[
            jax.ShapeDtypeStruct((tokens, dim), BF),
            jax.ShapeDtypeStruct((tokens, dim), F32),
            jax.ShapeDtypeStruct((states + 8, dim), BF),
        ],
        scratch_shapes=[pltpu.VMEM((tokens, cols), F32)],
        compiler_params=params(54),
        name="combine_and_scan",
    )(*tables, *backs, dout, delta, rate, total, mix, drive)


def reach_body(delta_ref, rate_ref, mix_ref, reach_ref, total_ref):
    delta = delta_ref[...]
    tokens, cols = delta.shape
    later = (
        lax.broadcasted_iota(jnp.int32, (tokens, tokens), 1)
        > lax.broadcasted_iota(jnp.int32, (tokens, tokens), 0)
    ).astype(F32)
    after = jnp.dot(
        later, delta, precision=lax.Precision.HIGHEST, preferred_element_type=F32
    )
    total_ref[...] = after[:1] + delta[:1]
    mix = mix_ref[...]
    for n in range(rate_ref.shape[0]):
        fade = jnp.exp(after * -jnp.broadcast_to(rate_ref[n : n + 1], (tokens, cols)))
        reach_ref[n] = (fade * jnp.broadcast_to(mix[:, n : n + 1], (tokens, cols))).astype(BF)


def reach_table(delta, rate, mix):
    tokens, dim = delta.shape
    states = rate.shape[0]
    cols = 512
    return pl.pallas_call(
        reach_body,
        grid=(dim // cols,),
        in_specs=[strip(tokens, cols), strip(states, cols), whole(*mix.shape)],
        out_specs=[
            pl.BlockSpec((states, tokens, cols), lambda i: (0, 0, i)),
            strip(1, cols),
        ],
        out_shape=[
            jax.ShapeDtypeStruct((states, tokens, dim), BF),
            jax.ShapeDtypeStruct((1, dim), F32),
        ],
        compiler_params=params(46),
        cost_estimate=pl.CostEstimate(
            flops=8 * states * tokens * dim,
            bytes_accessed=2 * states * tokens * dim,
            transcendentals=states * tokens * dim,
        ),
        name="reach_table",
    )(delta, rate, mix)


def carry_body(place_ref, starts_ref, rate_ref, local_ref, reach_ref, out_ref):
    place = place_ref[0]
    negative = -rate_ref[...]
    tokens, cols = local_ref.shape
    states = negative.shape[0]
    flow = jnp.zeros((states, cols), F32)
    for at in reversed(range(starts_ref.shape[0])):
        sent = starts_ref[at].astype(F32)
        total = sent[states : states + 1] + sent[states + 1 : states + 2]
        passed = jnp.exp(total * negative) * flow
        flow = jnp.where(at > place, sent[:states] + passed, flow)
    total = local_ref[...]
    for n in range(states):
        total += reach_ref[n].astype(F32) * flow[n : n + 1]
    out_ref[...] = total.astype(BF)


def add_carry(place, starts, rate, local, reach):
    tokens, dim = local.shape
    states = rate.shape[0]
    blocks = starts.shape[0]
    cols = SCAN_COLS
    return pl.pallas_call(
        carry_body,
        grid=(dim // cols,),
        in_specs=[
            pl.BlockSpec(memory_space=pltpu.SMEM),
            pl.BlockSpec((blocks, states + 8, cols), lambda i: (0, 0, i)),
            strip(states, cols),
            strip(tokens, cols),
            pl.BlockSpec((states, tokens, cols), lambda i: (0, 0, i)),
        ],
        out_specs=strip(tokens, cols),
        out_shape=jax.ShapeDtypeStruct((tokens, dim), BF),
        compiler_params=params(54),
        name="add_carry",
    )(place, starts, rate, local, reach)


def on_device(z_size, capacity, x_in, dout, route_ids, combine, w_up, w_down, delta, rate, bmat, cmat):
    experts = lax.axis_size("exp")
    x, dy, ids, weights = x_in[0], dout[0], route_ids[0], combine[0]
    up, down, steps = w_up[0], w_down[0], delta[0]

    def shift(value, by):
        ring = [(i, (i + by) % z_size) for i in range(z_size)]
        return lax.ppermute(value, "z", ring)

    def swap(value):
        return lax.ppermute(value, "core", [(0, 1), (1, 0)])

    def exchange(value):
        parts = value.reshape(experts, -1, value.shape[1])
        got = lax.all_to_all(parts, "exp", split_axis=0, concat_axis=0, tiled=True)
        return got.reshape(value.shape)

    sizes = part_sizes(capacity)
    sent = gather_rows(ids.T, x, dy, experts, capacity)
    up_other, down_other = swap(up), swap(down)
    got_low = exchange(sent[0])
    got_low, up_other, down_other = tie(got_low, up_other, down_other)
    both = (up, up_other, down, down_other)
    low = sort_messages(got_low, experts, sizes[0])
    got_high = exchange(sent[1])

    def ring(own):
        return shift(own, 1), shift(own, -1)

    def far(prev, next_):
        half = prev.shape[0] // 2
        return shift(prev[:half], 1), shift(next_[half:], -1)

    def some(part, count):
        return (sizes[part] * experts // 2,) * count

    low_near = ring(low)
    lanes = (steps.shape[0], bmat.shape[2], 128)
    mix = jnp.broadcast_to(bmat[0][:, :, None], lanes)
    drive = jnp.broadcast_to(cmat[0][:, :, None], lanes)
    reach, total = reach_table(steps, rate, bmat[0])
    tables = weigh_tables(ids, weights, experts, capacity)
    got_high, reach, total, tables, mix, drive = tie(
        got_high, reach, total, tables, mix, drive
    )
    high = sort_messages(got_high, experts, sizes[1])
    low_near, high = tie(low_near, high)
    low_far = far(*low_near)
    high_near = ring(high)
    first = expert_rows((low, *low_near, high), some(0, 3) + some(1, 1), both)
    low_far, high_near, first = tie(low_far, high_near, first)
    high_far = far(*high_near)
    second = expert_rows(low_far, some(0, 2), both)
    high_near, second = tie(high_near, second)
    third = expert_rows(high_near, some(1, 2), both)
    low_sums = hop_sums(*first[4:6], *first[2:4], shift(second[0], 1), shift(second[1], -1))
    high_far, third, low_sums = tie(high_far, third, low_sums)
    fourth = expert_rows(high_far, some(1, 2), both)

    def home(own, sums, size):
        to_next, to_prev = sums
        return pack_returns(*own, shift(to_next, 1), shift(to_prev, -1), size)

    low_home = home(first[:2], low_sums, sizes[0])
    high_got = (shift(fourth[0], 1), shift(fourth[1], -1))
    low_home, high_got = tie(low_home, high_got)
    low_back = exchange(low_home)
    high_sums = hop_sums(*third[2:4], *third[:2], *high_got)
    backs = (low_back, exchange(home(first[6:8], high_sums, sizes[1])))

    mid, local, start = combine_and_scan(
        tables, backs, dy, steps, rate, total, mix, drive
    )
    starts = lax.all_gather(start, ("z", "core"))
    place = lax.axis_index(("z", "core")).astype(jnp.int32).reshape(1)
    scan = add_carry(place, starts, rate, local, reach)
    return (mid[None], scan[None])


def solution(mesh):
    seq, exp = mesh.shape["seq"], mesh.shape["exp"]
    z_size = seq // CORES
    split = Mesh(mesh.devices.reshape(z_size, CORES, exp), ("z", "core", "exp"))
    token = P("exp", ("z", "core"), None)

    def run(x_in, dout, route_ids, *rest):
        tokens = route_ids.shape[1] // seq
        capacity = 5 * tokens * route_ids.shape[2] // (4 * exp)
        return jax.shard_map(
            functools.partial(on_device, z_size, capacity),
            mesh=split,
            in_specs=(token,) * 7 + (P(),) + (token,) * 2,
            out_specs=(token, token),
            check_vma=False,
        )(x_in, dout, route_ids, *rest)

    return run
```

```python
import functools

import jax
import jax.numpy as jnp
import numpy as np
from jax import lax
from jax.experimental import pallas as pl
from jax.experimental.pallas import tpu as pltpu
from jax.sharding import Mesh
from jax.sharding import PartitionSpec as P

CORES = 2
EARLY = 12
HIDDEN_STEP = 128
OUT_COLS = 512
SCAN_COLS = 1024
BF = jnp.bfloat16
F32 = jnp.float32


def params(mebibytes):
    return pltpu.CompilerParams(vmem_limit_bytes=mebibytes * 1024 * 1024)


def in_vmem(values):
    return [pltpu.with_memory_space_constraint(v, pltpu.VMEM) for v in values]


def whole(*shape):
    return pl.BlockSpec(shape, lambda *_: (0,) * len(shape))


def tie(*values):
    return lax.optimization_barrier(values)


def part_sizes(capacity):
    return (EARLY, capacity - EARLY)


def gather_body(capacity, ids_ref, x_ref, dy_ref, *outs):
    tokens = x_ref.shape[0]
    experts = outs[0].shape[0] // (2 * EARLY)
    ids = ids_ref[...]
    at = lax.broadcasted_iota(jnp.int32, (experts, tokens), 0)
    hots = [(at == ids[k : k + 1, :]).astype(F32) for k in range(2)]
    before = (
        lax.broadcasted_iota(jnp.int32, (tokens, tokens), 0)
        < lax.broadcasted_iota(jnp.int32, (tokens, tokens), 1)
    ).astype(F32)
    earlier = jnp.dot(
        (hots[0] + hots[1]).astype(BF), before.astype(BF), preferred_element_type=F32
    )
    slots = [
        jnp.sum(earlier * hot, axis=0, keepdims=True).astype(jnp.int32) for hot in hots
    ]
    first = 0
    for size, out in zip(part_sizes(capacity), outs):
        place = lax.broadcasted_iota(jnp.int32, (out.shape[0], tokens), 0)
        pick_x = pick_dy = None
        for k in range(2):
            slot = slots[k] - first
            inside = (slot >= 0) & (slot < size)
            target = jnp.where(inside, ids[k : k + 1, :] * (2 * size) + slot, -size - 1)
            hit_x, hit_dy = place == target, place == target + size
            pick_x = hit_x if pick_x is None else pick_x | hit_x
            pick_dy = hit_dy if pick_dy is None else pick_dy | hit_dy
        rows = jnp.dot(pick_x.astype(F32).astype(BF), x_ref[...], preferred_element_type=F32)
        rows += jnp.dot(
            pick_dy.astype(F32).astype(BF), dy_ref[...], preferred_element_type=F32
        )
        out[...] = rows.astype(BF)
        first += size


def gather_rows(ids_t, x, dy, experts, capacity):
    dim = x.shape[1]
    return pl.pallas_call(
        functools.partial(gather_body, capacity),
        out_shape=[
            jax.ShapeDtypeStruct((experts * 2 * size, dim), BF)
            for size in part_sizes(capacity)
        ],
        compiler_params=params(40),
        name="gather_rows",
    )(ids_t, x, dy)


def sort_body(table_ref, rows_ref, out):
    size = table_ref.shape[0]
    for low in range(0, out.shape[0], size):
        rows = rows_ref[low : low + size]
        out[low : low + size] = jnp.dot(
            table_ref[...], rows, preferred_element_type=F32
        ).astype(BF)


def sort_messages(messages, experts, size):
    count, dim = experts // 2, messages.shape[1]
    rows = 2 * size * count
    at = np.arange(rows)
    kind, rest = at // (size * count), at % (size * count)
    table = np.zeros((rows, rows), np.float32)
    table[at, rest // size * 2 * size + kind * size + rest % size] = 1.0
    return pl.pallas_call(
        sort_body,
        out_shape=jax.ShapeDtypeStruct((2 * rows, dim), BF),
        compiler_params=params(44),
        name="sort_messages",
    )(jnp.asarray(table, BF), *in_vmem((messages,)))


def padded(size):
    return -(-size // 8) * 8


def pack_body(spread, *refs):
    if spread:
        table_ref, refs = refs[0], refs[1:]
    own_a, own_b, prev_ref, next_ref, out = refs
    half = own_a.shape[0]
    sums = []
    for own, low in ((own_a, 0), (own_b, half)):
        total = own[...].astype(F32) + prev_ref[low : low + half].astype(F32)
        sums.append((total + next_ref[low : low + half].astype(F32)).astype(BF))
    rows = jnp.concatenate(sums, axis=0)
    if spread:
        rows = jnp.dot(table_ref[...], rows, preferred_element_type=F32).astype(BF)
    out[...] = rows


def pack_returns(own_a, own_b, from_prev, from_next, size):
    rows, dim = from_prev.shape
    wide = padded(size)
    spread = wide != size
    table = np.zeros((rows // size * wide, rows), np.float32)
    at = np.arange(rows)
    table[at // size * wide + at % size, at] = 1.0
    head = (jnp.asarray(table, BF),) if spread else ()
    return pl.pallas_call(
        functools.partial(pack_body, spread),
        out_shape=jax.ShapeDtypeStruct((rows // size * wide, dim), BF),
        compiler_params=params(16),
        name="pack_returns",
    )(*head, own_a, own_b, *in_vmem((from_prev, from_next)))


def hop_body(next_a, next_b, prev_a, prev_b, got_a, got_b, to_next, to_prev):
    half = next_a.shape[0]
    to_next[:half] = (next_a[...].astype(F32) + got_a[...].astype(F32)).astype(BF)
    to_next[half:] = next_b[...]
    to_prev[:half] = prev_a[...]
    to_prev[half:] = (prev_b[...].astype(F32) + got_b[...].astype(F32)).astype(BF)


def hop_sums(*parts):
    half, dim = parts[0].shape
    return pl.pallas_call(
        hop_body,
        out_shape=[jax.ShapeDtypeStruct((2 * half, dim), BF)] * 2,
        compiler_params=params(16),
        name="hop_sums",
    )(*parts[:4], *in_vmem(parts[4:]))


def expert_body(sizes, *refs):
    count = len(sizes)
    ins = refs[:count]
    up_a, up_b, down_a, down_b = refs[count : count + 4]
    outs = refs[count + 4 : -3]
    x_all, dy_all, grads = refs[-3:]
    hidden, dim = up_a.shape
    steps = hidden // HIDDEN_STEP
    low = 0
    for pieces, size in zip(ins, sizes):
        for top in range(0, pieces.shape[0], 2 * size):
            x_all[low : low + size] = pieces[top : top + size]
            dy_all[low : low + size] = pieces[top + size : top + 2 * size]
            low += size
    across = (((1,), (1,)), ((), ()))

    def step(i, carry):
        at = pl.ds(pl.multiple_of(i * HIDDEN_STEP, HIDDEN_STEP), HIDDEN_STEP)
        up = jnp.concatenate([up_a[at], up_b[at]], axis=0)
        down = jnp.concatenate([down_a[at], down_b[at]], axis=0)
        pre = lax.dot_general(x_all[...], up, across, preferred_element_type=F32)
        back = lax.dot_general(dy_all[...], down, across, preferred_element_type=F32)
        sig = jax.nn.sigmoid(pre)
        grad = (back * sig * (1.0 + pre * (1.0 - sig))).astype(BF)
        grads[0, i] = grad[:, :HIDDEN_STEP]
        grads[1, i] = grad[:, HIDDEN_STEP:]
        return carry

    lax.fori_loop(0, steps, step, 0)
    grad_a, grad_b = (
        jnp.concatenate([grads[core, i] for i in range(steps)], axis=1) for core in range(2)
    )
    for left in range(0, dim, OUT_COLS):
        cols = slice(left, left + OUT_COLS)
        part = jnp.dot(grad_a, up_a[:, cols], preferred_element_type=F32)
        part += jnp.dot(grad_b, up_b[:, cols], preferred_element_type=F32)
        part = part.astype(BF)
        low = 0
        for out in outs:
            size = out.shape[0]
            out[:, cols] = part[low : low + size]
            low += size


def expert_rows(ins, sizes, weights):
    dim = ins[0].shape[1]
    out_sizes = [
        size for value, size in zip(ins, sizes) for _ in range(value.shape[0] // (2 * size))
    ]
    rows = sum(out_sizes)
    hidden = weights[0].shape[0]
    vmem = pl.BlockSpec(memory_space=pltpu.VMEM)
    return pl.pallas_call(
        functools.partial(expert_body, sizes),
        in_specs=[vmem] * (len(ins) + 4),
        out_specs=[vmem] * len(out_sizes),
        out_shape=[jax.ShapeDtypeStruct((size, dim), BF) for size in out_sizes],
        scratch_shapes=[
            pltpu.VMEM((rows, dim), BF),
            pltpu.VMEM((rows, dim), BF),
            pltpu.VMEM((2, hidden // HIDDEN_STEP, rows, HIDDEN_STEP), BF),
        ],
        compiler_params=params(24),
        cost_estimate=pl.CostEstimate(
            flops=6 * rows * 2 * hidden * dim // 8,
            bytes_accessed=rows * dim,
            transcendentals=rows,
        ),
        name="expert_rows",
    )(*in_vmem(ins), *in_vmem(weights))


def weigh_pair(ids, weights, experts, capacity):
    tokens = ids.shape[0]
    at = lax.broadcasted_iota(jnp.int32, (tokens, experts), 1)
    hots = [(at == ids[:, k : k + 1]).astype(F32) for k in range(2)]
    before = (
        lax.broadcasted_iota(jnp.int32, (tokens, tokens), 1)
        < lax.broadcasted_iota(jnp.int32, (tokens, tokens), 0)
    ).astype(F32)
    earlier = jnp.dot(
        before.astype(BF), (hots[0] + hots[1]).astype(BF), preferred_element_type=F32
    )
    sizes = part_sizes(capacity)
    rows = experts * sum(padded(size) for size in sizes)
    place = lax.broadcasted_iota(jnp.int32, (tokens, rows), 1)
    table = jnp.zeros((tokens, rows), F32)
    for k in range(2):
        slot = jnp.sum(earlier * hots[k], axis=1, keepdims=True).astype(jnp.int32)
        own = ids[:, k : k + 1]
        target = jnp.where(
            slot < sizes[0],
            own * padded(sizes[0]) + slot,
            experts * padded(sizes[0]) + own * padded(sizes[1]) + slot - sizes[0],
        )
        table = table + jnp.where(place == target, weights[:, k : k + 1], 0.0)
    high = table.astype(BF)
    low = (table - high.astype(F32)).astype(BF)
    return high, low


def table_body(experts, capacity, ids_ref, weights_ref, high_ref, low_ref):
    high_ref[...], low_ref[...] = weigh_pair(
        ids_ref[...], weights_ref[...], experts, capacity
    )


def weigh_tables(ids, weights, experts, capacity):
    rows = experts * sum(padded(size) for size in part_sizes(capacity))
    return pl.pallas_call(
        functools.partial(table_body, experts, capacity),
        out_shape=[jax.ShapeDtypeStruct((ids.shape[0], rows), BF)] * 2,
        compiler_params=params(44),
        name="weigh_tables",
    )(ids, weights)


def fold_rows(parts):
    rows = lax.broadcasted_iota(jnp.int32, parts[0].shape, 0)
    for gap in (4, 2, 1):
        first = (rows & gap) == 0
        folded = []
        for a, b in zip(parts[:gap], parts[gap:]):
            kept, moved = jnp.where(first, a, b), jnp.where(first, b, a)
            if gap == 4:
                moved = pltpu.roll(moved, 4, 0)
            else:
                moved = jnp.where(first, pltpu.roll(moved, 8 - gap, 0), pltpu.roll(moved, gap, 0))
            folded.append(kept + moved)
        parts = folded
    return parts[0]


def scan_body(*refs):
    high_ref, low_ref = refs[:2]
    backs = refs[2:4]
    dout_ref, delta_ref, rate_ref, total_ref, mix_ref, drive_ref = refs[4:10]
    mid_ref, local_ref, start_ref, grad = refs[10:]
    back = jnp.concatenate([b[...] for b in backs], axis=0)
    routed = jnp.dot(high_ref[...], back, preferred_element_type=F32)
    routed += jnp.dot(low_ref[...], back, preferred_element_type=F32)
    mid = (dout_ref[...].astype(F32) + routed).astype(BF)
    mid_ref[...] = mid
    grad[...] = mid.astype(F32)
    negative = -rate_ref[...]
    tokens, cols = grad.shape
    states = negative.shape[0]
    repeat = cols // mix_ref.shape[2]

    def block(i, flow):
        low_t = pl.multiple_of((tokens // 8 - 1 - i) * 8, 8)
        grads = grad[pl.ds(low_t, 8)]
        deltas = delta_ref[pl.ds(low_t, 8)]
        rows = []
        for r in reversed(range(8)):
            drive = jnp.concatenate([drive_ref[low_t + r]] * repeat, axis=1)
            mix = jnp.concatenate([mix_ref[low_t + r]] * repeat, axis=1)
            state = drive * jnp.broadcast_to(grads[r : r + 1], (states, cols)) + flow
            product = mix * state
            rows.append(product[:8] + product[8:])
            decay = jnp.exp(jnp.broadcast_to(deltas[r : r + 1], (states, cols)) * negative)
            flow = decay * state
        local_ref[pl.ds(low_t, 8)] = fold_rows(rows[::-1])
        return flow

    flow = lax.fori_loop(0, tokens // 8, block, jnp.zeros((states, cols), F32), unroll=2)
    total = jnp.broadcast_to(total_ref[...], (8, cols))
    whole_part = total.astype(BF).astype(F32)
    row = lax.broadcasted_iota(jnp.int32, (8, cols), 0)
    tail = jnp.where(row == 0, whole_part, jnp.where(row == 1, total - whole_part, 0.0))
    start_ref[...] = jnp.concatenate([flow, tail], axis=0).astype(BF)


def strip(rows, cols):
    return pl.BlockSpec((rows, cols), lambda i: (0, i))


def combine_and_scan(tables, backs, dout, delta, rate, total, mix, drive):
    tokens, dim = dout.shape
    states = rate.shape[0]
    cols = SCAN_COLS
    return pl.pallas_call(
        scan_body,
        grid=(dim // cols,),
        in_specs=[whole(*t.shape) for t in tables]
        + [strip(b.shape[0], cols) for b in backs]
        + [
            strip(tokens, cols),
            strip(tokens, cols),
            strip(states, cols),
            strip(1, cols),
            whole(*mix.shape),
            whole(*drive.shape),
        ],
        out_specs=[strip(tokens, cols), strip(tokens, cols), strip(states + 8, cols)],
        out_shape=[
            jax.ShapeDtypeStruct((tokens, dim), BF),
            jax.ShapeDtypeStruct((tokens, dim), F32),
            jax.ShapeDtypeStruct((states + 8, dim), BF),
        ],
        scratch_shapes=[pltpu.VMEM((tokens, cols), F32)],
        compiler_params=params(54),
        name="combine_and_scan",
    )(*tables, *backs, dout, delta, rate, total, mix, drive)


def reach_body(delta_ref, rate_ref, mix_ref, reach_ref, total_ref):
    delta = delta_ref[...]
    tokens, cols = delta.shape
    later = (
        lax.broadcasted_iota(jnp.int32, (tokens, tokens), 1)
        > lax.broadcasted_iota(jnp.int32, (tokens, tokens), 0)
    ).astype(F32)
    after = jnp.dot(
        later, delta, precision=lax.Precision.HIGHEST, preferred_element_type=F32
    )
    total_ref[...] = after[:1] + delta[:1]
    mix = mix_ref[...]
    for n in range(rate_ref.shape[0]):
        fade = jnp.exp(after * -jnp.broadcast_to(rate_ref[n : n + 1], (tokens, cols)))
        reach_ref[n] = (fade * jnp.broadcast_to(mix[:, n : n + 1], (tokens, cols))).astype(BF)


def reach_table(delta, rate, mix):
    tokens, dim = delta.shape
    states = rate.shape[0]
    cols = 512
    return pl.pallas_call(
        reach_body,
        grid=(dim // cols,),
        in_specs=[strip(tokens, cols), strip(states, cols), whole(*mix.shape)],
        out_specs=[
            pl.BlockSpec((states, tokens, cols), lambda i: (0, 0, i)),
            strip(1, cols),
        ],
        out_shape=[
            jax.ShapeDtypeStruct((states, tokens, dim), BF),
            jax.ShapeDtypeStruct((1, dim), F32),
        ],
        compiler_params=params(46),
        cost_estimate=pl.CostEstimate(
            flops=8 * states * tokens * dim,
            bytes_accessed=2 * states * tokens * dim,
            transcendentals=states * tokens * dim,
        ),
        name="reach_table",
    )(delta, rate, mix)


def carry_body(place_ref, starts_ref, rate_ref, local_ref, reach_ref, out_ref):
    place = place_ref[0]
    negative = -rate_ref[...]
    tokens, cols = local_ref.shape
    states = negative.shape[0]
    flow = jnp.zeros((states, cols), F32)
    for at in reversed(range(starts_ref.shape[0])):
        sent = starts_ref[at].astype(F32)
        total = sent[states : states + 1] + sent[states + 1 : states + 2]
        passed = jnp.exp(total * negative) * flow
        flow = jnp.where(at > place, sent[:states] + passed, flow)
    total = local_ref[...]
    for n in range(states):
        total += reach_ref[n].astype(F32) * flow[n : n + 1]
    out_ref[...] = total.astype(BF)


def add_carry(place, starts, rate, local, reach):
    tokens, dim = local.shape
    states = rate.shape[0]
    blocks = starts.shape[0]
    cols = SCAN_COLS
    return pl.pallas_call(
        carry_body,
        grid=(dim // cols,),
        in_specs=[
            pl.BlockSpec(memory_space=pltpu.SMEM),
            pl.BlockSpec((blocks, states + 8, cols), lambda i: (0, 0, i)),
            strip(states, cols),
            strip(tokens, cols),
            pl.BlockSpec((states, tokens, cols), lambda i: (0, 0, i)),
        ],
        out_specs=strip(tokens, cols),
        out_shape=jax.ShapeDtypeStruct((tokens, dim), BF),
        compiler_params=params(54),
        name="add_carry",
    )(place, starts, rate, local, reach)


def on_device(z_size, capacity, x_in, dout, route_ids, combine, w_up, w_down, delta, rate, bmat, cmat):
    experts = lax.axis_size("exp")
    x, dy, ids, weights = x_in[0], dout[0], route_ids[0], combine[0]
    up, down, steps = w_up[0], w_down[0], delta[0]

    def shift(value, by):
        ring = [(i, (i + by) % z_size) for i in range(z_size)]
        return lax.ppermute(value, "z", ring)

    def swap(value):
        return lax.ppermute(value, "core", [(0, 1), (1, 0)])

    def exchange(value):
        parts = value.reshape(experts, -1, value.shape[1])
        got = lax.all_to_all(parts, "exp", split_axis=0, concat_axis=0, tiled=True)
        return got.reshape(value.shape)

    sizes = part_sizes(capacity)
    sent = gather_rows(ids.T, x, dy, experts, capacity)
    up_other, down_other = swap(up), swap(down)
    got_low = exchange(sent[0])
    got_low, up_other, down_other = tie(got_low, up_other, down_other)
    both = (up, up_other, down, down_other)
    low = sort_messages(got_low, experts, sizes[0])
    got_high = exchange(sent[1])

    def ring(own):
        return shift(own, 1), shift(own, -1)

    def far(prev, next_):
        half = prev.shape[0] // 2
        return shift(prev[:half], 1), shift(next_[half:], -1)

    def some(part, count):
        return (sizes[part] * experts // 2,) * count

    low_near = ring(low)
    lanes = (steps.shape[0], bmat.shape[2], 128)
    mix = jnp.broadcast_to(bmat[0][:, :, None], lanes)
    drive = jnp.broadcast_to(cmat[0][:, :, None], lanes)
    reach, total = reach_table(steps, rate, bmat[0])
    tables = weigh_tables(ids, weights, experts, capacity)
    got_high, reach, total, tables, mix, drive = tie(
        got_high, reach, total, tables, mix, drive
    )
    high = sort_messages(got_high, experts, sizes[1])
    low_near, high = tie(low_near, high)
    low_far = far(*low_near)
    high_near = ring(high)
    first = expert_rows((low, *low_near, high), some(0, 3) + some(1, 1), both)
    low_far, high_near, first = tie(low_far, high_near, first)
    high_far = far(*high_near)
    second = expert_rows(low_far, some(0, 2), both)
    high_near, second = tie(high_near, second)
    third = expert_rows(high_near, some(1, 2), both)
    low_sums = hop_sums(*first[4:6], *first[2:4], shift(second[0], 1), shift(second[1], -1))
    high_far, third, low_sums = tie(high_far, third, low_sums)
    fourth = expert_rows(high_far, some(1, 2), both)

    def home(own, sums, size):
        to_next, to_prev = sums
        return pack_returns(*own, shift(to_next, 1), shift(to_prev, -1), size)

    low_home = home(first[:2], low_sums, sizes[0])
    high_got = (shift(fourth[0], 1), shift(fourth[1], -1))
    low_home, high_got = tie(low_home, high_got)
    low_back = exchange(low_home)
    high_sums = hop_sums(*third[2:4], *third[:2], *high_got)
    backs = (low_back, exchange(home(first[6:8], high_sums, sizes[1])))

    mid, local, start = combine_and_scan(
        tables, backs, dy, steps, rate, total, mix, drive
    )
    starts = lax.all_gather(start, ("z", "core"))
    place = lax.axis_index(("z", "core")).astype(jnp.int32).reshape(1)
    scan = add_carry(place, starts, rate, local, reach)
    return (mid[None], scan[None])


def solution(mesh):
    seq, exp = mesh.shape["seq"], mesh.shape["exp"]
    z_size = seq // CORES
    split = Mesh(mesh.devices.reshape(z_size, CORES, exp), ("z", "core", "exp"))
    token = P("exp", ("z", "core"), None)

    def run(x_in, dout, route_ids, *rest):
        tokens = route_ids.shape[1] // seq
        capacity = 5 * tokens * route_ids.shape[2] // (4 * exp)
        return jax.shard_map(
            functools.partial(on_device, z_size, capacity),
            mesh=split,
            in_specs=(token,) * 7 + (P(),) + (token,) * 2,
            out_specs=(token, token),
            check_vma=False,
        )(x_in, dout, route_ids, *rest)

    return run
```
